32 devices in a mesh: groups: 2 (over y), gx: 16 (over z, x, core).
Axes of the slice: x: 2, y: 2, z: 4, core: 2. Of those that a mesh axis runs over, the one named last changes fastest.
Arguments:
- x_vec: float32 [1024, 8, 128], P(('groups', 'gx')), parts along dimension 0, may hold values from -6 to 6
- r_vec: float32 [1024, 8, 128], P(('groups', 'gx')), parts along dimension 0, may hold values from -40 to 40
- q_vec: float32 [1024, 8, 128], P(('groups', 'gx')), parts along dimension 0, may hold values from -40 to 40
- d_vec: float32 [1024, 8, 128], P(('groups', 'gx')), parts along dimension 0, may hold values from -6 to 6
- diag_blocks: bfloat16 [1024, 128, 128], P(('groups', 'gx')), parts along dimension 0, may hold values from -4 to 4
- off_blocks: bfloat16 [1024, 9, 128, 128], P(('groups', 'gx')), parts along dimension 0, may hold values from -1 to 1
- columns: int32 [1024, 9], P(('groups', 'gx')), parts along dimension 0, may hold values from 0 to 127
- colours: int32 [1024], P(('groups', 'gx')), parts along dimension 0, may hold values from 0 to 3
- factor_inv: bfloat16 [1024, 128, 128], P(('groups', 'gx')), parts along dimension 0, may hold values from -1 to 1, as said below
- pivot_diag: float32 [1024, 128], P(('groups', 'gx')), parts along dimension 0, may hold values from -2 to 2, as said below
- pivot_off: float32 [1024, 64], P(('groups', 'gx')), parts along dimension 0, may hold values from -1 to 1
- pivot_pairs: int32 [1024, 64], P(('groups', 'gx')), parts along dimension 0, may hold values 0 or 1
- face_lists: int32 [32, 6, 16], P(('groups', 'gx')), parts along dimension 0, may hold values from 0 to 31, as said below
- rho_prev: float32 [16], P('groups'), parts along dimension 0, may hold values from 0.5 to 2
- tau_prev: float32 [16], P('groups'), parts along dimension 0, may hold values from 0.5 to 2
- theta_prev: float32 [16], P('groups'), parts along dimension 0, may hold values from 0.2 to 2
Outputs:
- x_new: float32 [1024, 8, 128], P(('groups', 'gx')), parts along dimension 0
- r_new: float32 [1024, 8, 128], P(('groups', 'gx')), parts along dimension 0
- q_new: float32 [1024, 8, 128], P(('groups', 'gx')), parts along dimension 0
- d_new: float32 [1024, 8, 128], P(('groups', 'gx')), parts along dimension 0
- step_scalars: float32 [3, 16], P(None, 'groups'), parts along dimension 1
The draws below stay inside these ranges and needn't reach their ends.
There are 2 independent parts, one for each index of `groups`. The reference program is written for one: setup_inputs(seed, part) draws one part's arguments, and reference() takes and returns one part's arrays. A program takes and returns all parts, laid end to end along the dimension named above; each array names one. Nothing has to cross between parts.
Inputs may be any that keep to these rules, and one draw needn't show every extreme that they name: `columns`: column values below 32 name a block of the same tile; a value 32 + f * 16 + s names entry s of face list f of the tile that face f reaches. `face_lists`: each face list holds 16 different local block numbers of its tile. `factor_inv`: unit lower triangular: ones on the diagonal, zeros above it. `pivot_diag`: entries at even positions are positive, at odd positions negative; magnitudes 0.5 to 2.
All inputs are finite; a program needn't handle non-finite values. No bound on the sum of `pivot_pairs` on one device may be relied on, other than what follows from the above.
Results may differ from the reference program's by a relative error of at most 0.0053.
Values may be sent and summed in bfloat16 or wider, within the bound.
No kernel may reach another device: no remote copies, remote signals or barrier semaphores. Data moves between devices by JAX's collectives and lax.ppermute only.
A program may use at most 64 MiB of HBM per device.

```python
import math
import jax
import jax.numpy as jnp
from jax import lax

B = 128
NRHS = 8
K = 9
BLK_DEV = 32
FACE = 16
NBLK = 512
N_GX = 16


def ramp_rows(rows):
    position = jnp.arange(rows, dtype=jnp.float32) / max(rows - 1, 1)
    return jnp.exp(math.log(3.0) * position)


def draw_r_vec(key, part):
    key = jax.random.fold_in(key, 22)
    first = jax.random.fold_in(key, 0)
    second = jax.random.fold_in(key, 1)
    fourth = jax.random.fold_in(key, 3)
    base = jnp.clip(jax.random.normal(first, (NBLK, NRHS, B)), -5.0, 5.0)
    level = jax.random.uniform(fourth, (NBLK, 1, 1), minval=0.5, maxval=1.5)
    scales = jnp.exp(jax.random.uniform(second, (NRHS,), minval=math.log(0.5), maxval=math.log(2.0)))
    pattern = jnp.where(jnp.arange(B) % 2 == 0, 1.0, -1.0)[None, None, :]
    total = base * scales[None, :, None] + level * pattern
    return (total * ramp_rows(NBLK)[:, None, None]).astype(jnp.float32)


def draw_q_vec(key, part):
    key = jax.random.fold_in(key, 21)
    first, second = jax.random.split(key, 2)
    base = jnp.clip(jax.random.normal(first, (NBLK, NRHS, B)), -5.0, 5.0)
    scales = jnp.exp(jax.random.uniform(second, (2, NRHS), minval=math.log(0.5), maxval=math.log(2.0)))
    even = (jnp.arange(B) % 2 == 0)[None, None, :]
    column = jnp.where(even, scales[0][None, :, None], scales[1][None, :, None])
    return (base * column * ramp_rows(NBLK)[:, None, None]).astype(jnp.float32)


def draw_diag_blocks(key, part):
    key = jax.random.fold_in(key, 23)
    noise = jnp.clip(jax.random.normal(key, (NBLK, B, B)), -5.0, 5.0)
    noise = noise * (0.5 / math.sqrt(B))
    signs = jnp.where(jnp.arange(B) % 2 == 0, 3.0, -1.0)
    return (noise + jnp.eye(B, dtype=jnp.float32)[None] * signs[None, None, :]).astype(jnp.bfloat16)


def draw_off_blocks(key, part):
    key = jax.random.fold_in(key, 27)
    noise = jnp.clip(jax.random.normal(key, (NBLK, K, B, B)), -5.0, 5.0)
    spread = 1.0 / math.sqrt(K * B)
    shift = 0.6 / (K * B)
    return (noise * spread + shift).astype(jnp.bfloat16)


def draw_factor_inv(key, part):
    key = jax.random.fold_in(key, 24)
    noise = jnp.clip(jax.random.normal(key, (NBLK, B, B)), -5.0, 5.0)
    noise = noise * (0.5 / math.sqrt(B))
    lower = (jnp.arange(B)[:, None] > jnp.arange(B)[None, :]).astype(jnp.float32)
    return (noise * lower[None] + jnp.eye(B, dtype=jnp.float32)[None]).astype(jnp.bfloat16)


def draw_pivot_diag(key, part):
    key = jax.random.fold_in(key, 25)
    size = jax.random.uniform(key, (NBLK, B), minval=0.5, maxval=2.0)
    signs = jnp.where(jnp.arange(B) % 2 == 0, 1.0, -1.0)
    return (size * signs[None, :]).astype(jnp.float32)


def draw_face_lists(key, part):
    key = jax.random.fold_in(key, 26)
    keys = jax.random.split(key, N_GX * 6)
    orders = jax.vmap(lambda single: jax.random.permutation(single, BLK_DEV))(keys)
    return orders[:, :FACE].reshape(N_GX, 6, FACE).astype(jnp.int32)


def place_ends(entries, rng, smallest, top_value):
    dims = entries.shape
    place = [jax.random.randint(jax.random.fold_in(rng, axis), (), 0, dims[axis]) for axis in range(len(dims))]
    entries = entries.at[tuple(place)].set(smallest)
    longest = dims.index(max(dims))
    place[longest] = (place[longest] + 1) % dims[longest]
    return entries.at[tuple(place)].set(top_value)


def level_of(stream_key, shape, cuts, least, top_value):
    level = 1.0
    for dim, shards_of in cuts:
        draws = jax.random.uniform(jax.random.fold_in(jax.random.fold_in(stream_key, 6), dim), (shards_of,), jnp.float32, least / len(cuts), top_value / len(cuts))
        level = level * jnp.repeat(jnp.exp(draws), shape[dim] // shards_of).reshape((-1,) + (1,) * (len(shape) - 1 - dim))
    return level


def centred(key, dims, deviation, bound, shards=(), kind=jnp.bfloat16):
    level = level_of(key, dims, shards, -0.22, 0.18) if shards else 1.0
    values = jax.random.normal(key, dims, jnp.float32) * deviation * level
    return jnp.minimum(jnp.maximum(values, -bound), bound).astype(kind)


def setup_inputs(seed: int = 0, part: int = 0) -> dict:
    streams_of = jax.random.split(jax.random.key(seed), 17)
    own_keys = jax.random.split(jax.random.fold_in(streams_of[16], part), 17)
    x_vec = centred(own_keys[0], (NBLK, NRHS, B), 1.0, 6.0, ((0, 16),), jnp.float32)
    r_vec = draw_r_vec(jax.random.fold_in(jax.random.fold_in(streams_of[16], part), 71), part)
    q_vec = draw_q_vec(jax.random.fold_in(jax.random.fold_in(streams_of[16], part), 71), part)
    d_vec = centred(own_keys[3], (NBLK, NRHS, B), 1.0, 6.0, ((0, 16),), jnp.float32)
    diag_blocks = draw_diag_blocks(jax.random.fold_in(jax.random.fold_in(streams_of[16], part), 71), part)
    off_blocks = draw_off_blocks(jax.random.fold_in(jax.random.fold_in(streams_of[16], part), 71), part)
    columns = place_ends(jax.random.randint(own_keys[6], (NBLK, K), 0, 4 * BLK_DEV), jax.random.fold_in(own_keys[6], 1), 0, (4 * BLK_DEV) - 1).astype(jnp.int32)
    colours = place_ends(jax.random.randint(own_keys[7], (NBLK,), 0, 4), jax.random.fold_in(own_keys[7], 1), 0, 3).astype(jnp.int32)
    factor_inv = draw_factor_inv(jax.random.fold_in(jax.random.fold_in(streams_of[16], part), 71), part)
    pivot_diag = draw_pivot_diag(jax.random.fold_in(jax.random.fold_in(streams_of[16], part), 71), part)
    pivot_off = jnp.clip(jax.random.uniform(own_keys[10], (NBLK, B // 2), jnp.float32, -1.0, 1.0) * level_of(own_keys[10], (NBLK, B // 2), ((0, 16),), -0.4, 0.0), -1.0, 1.0)
    pivot_pairs = place_ends((jax.random.randint(own_keys[11], (NBLK, B // 2), 0, 2) < 1).astype(jnp.int32), jax.random.fold_in(own_keys[11], 1), 0, 1)
    face_lists = draw_face_lists(jax.random.fold_in(jax.random.fold_in(streams_of[16], part), 71), part)
    rho_prev = jnp.clip(jnp.exp(jax.random.uniform(own_keys[13], (NRHS,), jnp.float32, math.log(0.5), math.log(2.0))), 0.5, 2.0)
    tau_prev = jnp.clip(jnp.exp(jax.random.uniform(own_keys[14], (NRHS,), jnp.float32, math.log(0.5), math.log(2.0))), 0.5, 2.0)
    theta_prev = jnp.clip(jnp.exp(jax.random.uniform(own_keys[15], (NRHS,), jnp.float32, math.log(0.2), math.log(2.0))), 0.2, 2.0)
    return dict(x_vec=x_vec, r_vec=r_vec, q_vec=q_vec, d_vec=d_vec, diag_blocks=diag_blocks, off_blocks=off_blocks, columns=columns, colours=colours, factor_inv=factor_inv, pivot_diag=pivot_diag, pivot_off=pivot_off, pivot_pairs=pivot_pairs, face_lists=face_lists, rho_prev=rho_prev, tau_prev=tau_prev, theta_prev=theta_prev)


OFFSETS = (1, -1, 4, -4, 16, -16)

def couplings(columns, face_lists):
    tiles = (jnp.arange(NBLK) // BLK_DEV).astype(jnp.int32)
    tz = tiles % 4
    ty = tiles // 4 % 4
    tx = tiles // 16
    conds = jnp.stack([tz != 0, tz != 3, ty != 0, ty != 3, tx != 0, tx != N_GX // 16 - 1], axis=1)
    offs = jnp.array(OFFSETS, dtype=jnp.int32)
    rel = columns - BLK_DEV
    face = jnp.clip(rel // FACE, 0, 5).astype(jnp.int32)
    slot = (rel % FACE).astype(jnp.int32)
    source = jnp.clip(tiles[:, None] - offs[face], 0, N_GX - 1).astype(jnp.int32)
    remote = source * BLK_DEV + face_lists[source, face, slot]
    local = tiles[:, None] * BLK_DEV + columns
    is_local = columns < BLK_DEV
    present = jnp.take_along_axis(conds, face, axis=1)
    index = jnp.where(is_local, local, remote).astype(jnp.int32)
    keep = jnp.where(is_local, True, present)
    return (index, keep)

def pivot_solve(values, pivot_diag, pivot_off, pivot_pairs):
    rows, count, width = values.shape
    half = width // 2
    pairs = values.reshape(rows, count, half, 2)
    first, second = (pairs[..., 0], pairs[..., 1])
    diag = pivot_diag.reshape(rows, 1, half, 2)
    d_one, d_two = (diag[..., 0], diag[..., 1])
    off = pivot_off[:, None, :]
    paired = pivot_pairs[:, None, :] == 1
    det = d_one * d_two - off * off
    out_one = jnp.where(paired, (d_two * first - off * second) / det, first / d_one)
    out_two = jnp.where(paired, (d_one * second - off * first) / det, second / d_two)
    return jnp.stack([out_one, out_two], axis=-1).reshape(rows, count, width)

def reference(x_vec, r_vec, q_vec, d_vec, diag_blocks, off_blocks, columns, colours, factor_inv, pivot_diag, pivot_off, pivot_pairs, face_lists, rho_prev, tau_prev, theta_prev):
    index, keep = couplings(columns, face_lists)
    off_tiles = off_blocks.reshape(N_GX, BLK_DEV, K, B, B)
    index_tiles = index.reshape(N_GX, BLK_DEV, K)
    keep_tiles = keep.astype(jnp.float32).reshape(N_GX, BLK_DEV, K)
    factor = factor_inv.astype(jnp.float32)

    def couple(values):

        def one(item):
            blocks, rows, weight = item
            gathered = jnp.take(values, rows, axis=0).astype(jnp.float32) * weight[:, :, None, None]
            return jnp.einsum('iknb,ikab->ina', gathered, blocks.astype(jnp.float32))
        return lax.map(one, (off_tiles, index_tiles, keep_tiles)).reshape(NBLK, NRHS, B)

    def apply_dinv(vector):
        first = jnp.einsum('inb,iab->ina', vector.astype(jnp.bfloat16).astype(jnp.float32), factor)
        middle = pivot_solve(first, pivot_diag, pivot_off, pivot_pairs).astype(jnp.bfloat16)
        return jnp.einsum('inb,iba->ina', middle.astype(jnp.float32), factor)
    count = NBLK * B
    q_bf = q_vec.astype(jnp.bfloat16)
    image = jnp.einsum('inb,iab->ina', q_bf.astype(jnp.float32), diag_blocks.astype(jnp.float32)) + couple(q_bf)
    sigma = lax.optimization_barrier(jnp.sum(q_vec * image, axis=(0, 2))) / count
    sigma_safe = jnp.where(sigma >= 0, jnp.maximum(sigma, 0.5), jnp.minimum(sigma, -0.5))
    alpha = rho_prev / sigma_safe
    r_new = r_vec - alpha[None, :, None] * image
    norm_sq = lax.optimization_barrier(jnp.sum(r_new * r_new, axis=(0, 2))) / count
    theta = jnp.sqrt(norm_sq + 1e-06) / tau_prev
    csq = 1.0 / (1.0 + theta * theta)
    tau_new = tau_prev * theta * jnp.sqrt(csq)
    d_new = (csq * theta_prev * theta_prev)[None, :, None] * d_vec + (csq * alpha)[None, :, None] * q_vec
    x_new = x_vec + d_new
    sweep = jnp.zeros_like(r_new)
    for colour in range(4):
        chosen = (colours == colour)[:, None, None]
        update = apply_dinv(r_new - couple(sweep.astype(jnp.bfloat16)))
        sweep = jnp.where(chosen, update, sweep)
    back = jnp.zeros_like(r_new)
    for colour in (3, 2, 1, 0):
        chosen = (colours == colour)[:, None, None]
        update = sweep - apply_dinv(couple(back.astype(jnp.bfloat16)))
        back = jnp.where(chosen, update, back)
    rho_new = lax.optimization_barrier(jnp.sum(r_new * back, axis=(0, 2))) / count
    beta = rho_new / rho_prev
    q_new = back + beta[None, :, None] * q_vec
    return (x_new, r_new, q_new, d_new, jnp.stack([rho_new, tau_new, theta]))
```

```python
import functools

import jax
import jax.numpy as jnp
from jax import lax
from jax.experimental import pallas as pl
from jax.experimental.pallas import tpu as pltpu
from jax.sharding import PartitionSpec as P

F32 = jnp.float32
BF16 = jnp.bfloat16
VMEM = pltpu.VMEM
SMEM = pltpu.SMEM
SIDE = 4
UNROLL = 4


def swap_pairs(stride, extent, phase, tiles):
    pairs = []
    for tile in range(tiles):
        place = tile // stride % extent
        if place % 2 == phase and place + 1 < extent:
            pairs += [(tile, tile + stride), (tile + stride, tile)]
    return pairs


def swaps_of(tiles):
    swaps = []
    for axis, (stride, extent) in enumerate(((1, SIDE), (SIDE, SIDE), (16, tiles // 16))):
        for phase in range(2):
            pairs = swap_pairs(stride, extent, phase, tiles)
            if pairs:
                swaps.append((axis, phase, pairs))
    return swaps


def going_up(axis, phase):
    place = lax.axis_index("gx") // (1, SIDE, 16)[axis]
    return jnp.where(lax.rem(place, 2) == phase, 1, 0)


def send_faces(swaps, state, faces, sent):
    for (axis, phase, _), out in zip(swaps, sent):
        face = 2 * axis + 1 - going_up(axis, phase)
        for slot in range(0, 16, 2):
            two = [state[faces[0, face, slot + j]] for j in range(2)]
            rows = pl.ds(slot * 8, 16)
            out[rows, :] = jnp.concatenate(two, axis=0).astype(BF16)


def take_faces(swaps, arrived, extended):
    for (axis, phase, _), piece in zip(swaps, arrived):
        face = 2 * axis + going_up(axis, phase)
        extended[pl.ds(32 + face * 16, 16)] = piece[...].astype(F32).reshape(16, 8, 128)


def dot_t(left, right):
    return lax.dot_general(left, right, (((1,), (1,)), ((), ())), preferred_element_type=F32)


def coupled(block, extended, off, columns):
    total = None
    for k in range(9):
        term = dot_t(extended[columns[block, k]].astype(BF16), off[block, k])
        total = term if total is None else total + term
    return total


def solved(block, vector, factor, straight, crossed):
    matrix = factor[block]
    first = dot_t(vector.astype(BF16), matrix)
    lane = lax.broadcasted_iota(jnp.int32, first.shape, 1)
    other = jnp.where(lane % 2 == 0, pltpu.roll(first, 127, 1), pltpu.roll(first, 1, 1))
    row = pl.ds(block, 1)
    middle = straight[row, :] * first + crossed[row, :] * other
    return jnp.dot(middle.astype(BF16), matrix, preferred_element_type=F32)


def for_colour(colour, tables, body):
    count = tables[4, colour]

    def step(group, carry):
        body([tables[colour, group * UNROLL + j] for j in range(UNROLL)])
        return carry

    lax.fori_loop(0, (count + UNROLL - 1) // UNROLL, step, 0)


def first_kernel(swaps, q_ref, faces_in, faces, *sent):
    for face in range(6):
        for slot in range(16):
            faces[0, face, slot] = faces_in[0, face, slot]
    send_faces(swaps, q_ref, faces_in, sent)


def setup_kernel(columns_in, colours_in, diag_ref, off_ref, pairs_ref, columns, tables, straight, crossed):
    def copy_row(row, carry):
        for k in range(9):
            columns[row, k] = columns_in[row, k]
        return carry

    lax.fori_loop(0, 32, copy_row, 0)
    for colour in range(4):
        count = jnp.int32(0)
        for block in range(32):
            tables[colour, count] = block
            count = count + jnp.where(colours_in[block] == colour, 1, 0)
        last = tables[colour, jnp.maximum(count - 1, 0)]
        for j in range(UNROLL):
            tables[colour, count + j] = last
        tables[4, colour] = count
    half = lax.broadcasted_iota(jnp.int32, (64, 128), 0)
    lane = lax.broadcasted_iota(jnp.int32, (64, 128), 1)
    spread = jnp.where(lane // 2 == half, 1.0, 0.0).astype(F32)
    off = jnp.dot(off_ref[...], spread, precision=lax.Precision.HIGHEST, preferred_element_type=F32)
    paired = jnp.dot(
        pairs_ref[...].astype(F32), spread, precision=lax.Precision.HIGHEST, preferred_element_type=F32
    )
    own = diag_ref[...]
    even = lax.broadcasted_iota(jnp.int32, own.shape, 1) % 2 == 0
    other = jnp.where(even, pltpu.roll(own, 127, 1), pltpu.roll(own, 1, 1))
    det = own * other - off * off
    straight[...] = jnp.where(paired > 0.5, other / det, 1.0 / own)
    crossed[...] = jnp.where(paired > 0.5, -off / det, 0.0)


def image_kernel(swaps, tiles, q_ref, diag, off, columns, *refs):
    arrived, (image, partial, extended) = refs[: len(swaps)], refs[len(swaps) :]
    extended[pl.ds(0, 32)] = q_ref[...].astype(BF16).astype(F32)
    extended[pl.ds(32, 96)] = jnp.zeros((96, 8, 128), F32)
    take_faces(swaps, arrived, extended)

    def step(group, total):
        for j in range(UNROLL):
            block = group * UNROLL + j
            value = dot_t(extended[block].astype(BF16), diag[block])
            value = value + coupled(block, extended, off, columns)
            image[block] = value
            total = total + q_ref[block] * value
        return total

    total = lax.fori_loop(0, 32 // UNROLL, step, jnp.zeros((8, 128), F32))
    for tile in range(tiles):
        partial[tile] = total


def column_of(values):
    row = lax.broadcasted_iota(jnp.int32, (8, 128), 0)
    out = jnp.zeros((8, 128), F32)
    for n in range(8):
        out = jnp.where(row == n, values[n], out)
    return out


def start_kernel(
    swaps, count, sums, r_ref, image, rho, factor, straight, crossed, tables, faces, r_new, w, norm, alpha, *sent
):
    sigma = jnp.sum(jnp.sum(sums[...], axis=0), axis=1, keepdims=True) / count
    sigma = jnp.where(sigma >= 0, jnp.maximum(sigma, 0.5), jnp.minimum(sigma, -0.5))
    step_size = column_of(rho) / sigma
    alpha[...] = step_size
    new = r_ref[...] - step_size[None] * image[...]
    r_new[...] = new
    norm[...] = jnp.sum(new * new, axis=0)
    w[...] = jnp.zeros_like(w)

    def body(blocks):
        values = [solved(b, r_new[b], factor, straight, crossed) for b in blocks]
        for b, value in zip(blocks, values):
            w[b] = value

    for_colour(0, tables, body)
    send_faces(swaps, w, faces, sent)


def forward_kernel(swaps, colour, r_new, w_in, off, factor, straight, crossed, columns, tables, faces, *refs):
    n = len(swaps)
    arrived, w, sent, extended = refs[:n], refs[n], refs[n + 1 : -1], refs[-1]
    w[...] = w_in[...]
    extended[pl.ds(0, 32)] = w_in[...].astype(BF16).astype(F32)
    extended[pl.ds(32, 96)] = jnp.zeros((96, 8, 128), F32)
    take_faces(swaps, arrived, extended)

    def body(blocks):
        rest = [r_new[b] - coupled(b, extended, off, columns) for b in blocks]
        values = [solved(b, s, factor, straight, crossed) for b, s in zip(blocks, rest)]
        for b, value in zip(blocks, values):
            w[b] = value

    for_colour(colour, tables, body)
    if colour == 3:
        z = sent[0]
        z[...] = jnp.zeros_like(z)

        def copy(blocks):
            for b in blocks:
                z[b] = w[b]

        for_colour(3, tables, copy)
        send_faces(swaps, z, faces, sent[1:])
    else:
        send_faces(swaps, w, faces, sent)


def backward_kernel(swaps, tiles, colour, w, z_in, off, factor, straight, crossed, columns, tables, faces, *refs):
    n = len(swaps)
    arrived, rest = refs[:n], refs[n:]
    if colour == 0:
        r_new, norm, z, partial, extended = rest
    else:
        z, sent, extended = rest[0], rest[1:-1], rest[-1]
    z[...] = z_in[...]
    extended[pl.ds(0, 32)] = z_in[...].astype(BF16).astype(F32)
    extended[pl.ds(32, 96)] = jnp.zeros((96, 8, 128), F32)
    take_faces(swaps, arrived, extended)

    def body(blocks):
        sums = [coupled(b, extended, off, columns) for b in blocks]
        values = [w[b] - solved(b, s, factor, straight, crossed) for b, s in zip(blocks, sums)]
        for b, value in zip(blocks, values):
            z[b] = value

    for_colour(colour, tables, body)
    if colour == 0:
        rho = jnp.sum(r_new[...] * z[...], axis=0)
        both = jnp.concatenate([rho, norm[...]], axis=0)
        for tile in range(tiles):
            partial[tile] = both
    else:
        send_faces(swaps, z, faces, sent)


def last_kernel(count, sums, z, q_ref, x_ref, d_ref, alpha, rho, tau, theta_in, x_new, q_new, d_new, scalars):
    both = jnp.sum(jnp.sum(sums[...], axis=0), axis=1, keepdims=True) / count
    rho_new = both[:8] + jnp.zeros((8, 128), F32)
    norm = both[8:]
    tau_old = column_of(tau)
    theta_old = column_of(theta_in)
    theta = jnp.sqrt(norm + 1e-06) / tau_old
    csq = 1.0 / (1.0 + theta * theta)
    tau_new = tau_old * theta * jnp.sqrt(csq)
    beta = rho_new / column_of(rho)
    q_old = q_ref[...]
    d = (csq * theta_old * theta_old)[None] * d_ref[...] + (csq * alpha[...])[None] * q_old
    d_new[...] = d
    x_new[...] = x_ref[...] + d
    q_new[...] = z[...] + beta[None] * q_old
    row = lax.broadcasted_iota(jnp.int32, (8, 128), 0)
    lane = lax.broadcasted_iota(jnp.int32, (8, 128), 1)
    for index, value in enumerate((rho_new, tau_new, theta)):
        line = jnp.sum(jnp.where(row == lane, value, 0.0), axis=0, keepdims=True)
        scalars[pl.ds(index, 1), :] = line[:, :8]


def vec(*shape, dtype=F32):
    return jax.ShapeDtypeStruct(shape, dtype)


def call(body, outs, places, scratch=()):
    return pl.pallas_call(
        body,
        out_shape=outs,
        in_specs=[pl.BlockSpec(memory_space=place) for place in places],
        out_specs=[pl.BlockSpec(memory_space=getattr(out, "memory_space", VMEM)) for out in outs],
        scratch_shapes=list(scratch),
        compiler_params=pltpu.CompilerParams(vmem_limit_bytes=16 * 2**20),
    )


def per_device(
    x_vec,
    r_vec,
    q_vec,
    d_vec,
    diag_blocks,
    off_blocks,
    columns,
    colours,
    factor_inv,
    pivot_diag,
    pivot_off,
    pivot_pairs,
    face_lists,
    rho_prev,
    tau_prev,
    theta_prev,
):
    tiles = lax.axis_size("gx")
    swaps = swaps_of(tiles)
    n = len(swaps)
    count = float(q_vec.shape[0] * q_vec.shape[2] * tiles)
    block_vec = vec(32, 8, 128)
    pieces = [vec(128, 128, dtype=BF16)] * n
    scratch = [VMEM((128, 8, 128), F32)]

    def exchange(sent):
        return [lax.ppermute(piece, "gx", pairs) for piece, (_, _, pairs) in zip(sent, swaps)]

    faces, *sent = call(
        functools.partial(first_kernel, swaps),
        [SMEM((1, 6, 16), jnp.int32)] + pieces,
        [VMEM, SMEM],
    )(q_vec, face_lists)
    arrived = exchange(sent)
    columns, tables, straight, crossed = call(
        setup_kernel,
        [SMEM((32, 9), jnp.int32), SMEM((8, 128), jnp.int32), vec(32, 128), vec(32, 128)],
        [SMEM, SMEM, VMEM, VMEM, VMEM],
    )(columns, colours, pivot_diag, pivot_off, pivot_pairs)
    image, partial = call(
        functools.partial(image_kernel, swaps, tiles),
        [block_vec, vec(tiles, 8, 128)],
        [VMEM] * 3 + [SMEM] + [VMEM] * n,
        scratch,
    )(q_vec, diag_blocks, off_blocks, columns, *arrived)
    sums = lax.all_to_all(partial, "gx", 0, 0, tiled=True)
    r_new, w, norm, alpha, *sent = call(
        functools.partial(start_kernel, swaps, count),
        [block_vec, block_vec, vec(8, 128), vec(8, 128)] + pieces,
        [VMEM] * 3 + [SMEM] + [VMEM] * 3 + [SMEM] * 2,
    )(sums, r_vec, image, rho_prev, factor_inv, straight, crossed, tables, faces)
    fixed = (off_blocks, factor_inv, straight, crossed, columns, tables, faces)
    fixed_places = [VMEM] * 4 + [SMEM] * 3
    for colour in (1, 2, 3):
        w, *sent = call(
            functools.partial(forward_kernel, swaps, colour),
            [block_vec] * (2 if colour == 3 else 1) + pieces,
            [VMEM] * 2 + fixed_places + [VMEM] * n,
            scratch,
        )(r_new, w, *fixed, *exchange(sent))
    z, *sent = sent
    for colour in (2, 1):
        z, *sent = call(
            functools.partial(backward_kernel, swaps, tiles, colour),
            [block_vec] + pieces,
            [VMEM] * 2 + fixed_places + [VMEM] * n,
            scratch,
        )(w, z, *fixed, *exchange(sent))
    z, partial = call(
        functools.partial(backward_kernel, swaps, tiles, 0),
        [block_vec, vec(tiles, 16, 128)],
        [VMEM] * 2 + fixed_places + [VMEM] * (n + 2),
        scratch,
    )(w, z, *fixed, *exchange(sent), r_new, norm)
    sums = lax.all_to_all(partial, "gx", 0, 0, tiled=True)
    x_new, q_new, d_new, scalars = call(
        functools.partial(last_kernel, count),
        [block_vec] * 3 + [vec(3, 8)],
        [VMEM] * 6 + [SMEM] * 3,
    )(sums, z, q_vec, x_vec, d_vec, alpha, rho_prev, tau_prev, theta_prev)
    return (x_new, r_new, q_new, d_new, scalars)


def solution(mesh):
    blocks = P(("groups", "gx"))
    return jax.shard_map(
        per_device,
        mesh=mesh,
        in_specs=(blocks,) * 13 + (P("groups"),) * 3,
        out_specs=(blocks,) * 4 + (P(None, "groups"),),
        check_vma=False,
    )
```

```python
import functools

import jax
import jax.numpy as jnp
from jax import lax
from jax.experimental import pallas as pl
from jax.experimental.pallas import tpu as pltpu
from jax.sharding import PartitionSpec as P

F32 = jnp.float32
BF16 = jnp.bfloat16
VMEM = pltpu.VMEM
SMEM = pltpu.SMEM
HBM = pltpu.HBM
SIDE = 4
COUPLE = 4
SOLVE = 16


def swap_pairs(axis, stride, extent, phase, tiles):
    pairs = []
    for tile in range(tiles):
        place = tile // stride % extent
        up = place % 2 == phase
        other = place + 1 if up else place - 1
        if 0 <= other < extent:
            pairs.append((tile, tile + (other - place) * stride))
        elif axis == 0:
            pairs.append((tile, tile + (extent - 1 - 2 * place) * stride))
        else:
            pairs.append((tile, tile ^ 1))
    return pairs


def swaps_of(tiles):
    swaps = []
    for axis, (stride, extent) in enumerate(((1, SIDE), (SIDE, SIDE), (16, tiles // 16))):
        for phase in range(2 if extent > 2 else extent - 1):
            swaps.append((axis, phase, extent, swap_pairs(axis, stride, extent, phase, tiles)))
    return swaps


def partner(axis, phase, extent):
    place = lax.rem(lax.axis_index("gx") // (1, SIDE, 16)[axis], extent)
    up = jnp.where(lax.rem(place, 2) == phase, 1, 0)
    other = place + 2 * up - 1
    return up, (other >= 0) & (other < extent)


def send_faces(swaps, state, faces, sent):
    for (axis, phase, extent, _), out in zip(swaps, sent):
        up, _ = partner(axis, phase, extent)
        face = 2 * axis + 1 - up
        for slot in range(0, 16, 2):
            two = [state[faces[face, 0, slot + j]] for j in range(2)]
            out[pl.ds(slot * 8, 16), :] = jnp.concatenate(two, axis=0).astype(BF16)


def extend(swaps, state, arrived, extended):
    extended[pl.ds(0, 32)] = state[...].astype(BF16).astype(F32)
    zeros = jnp.zeros((16, 8, 128), F32)
    reached = set()
    for (axis, phase, extent, _), piece in zip(swaps, arrived):
        up, real = partner(axis, phase, extent)
        value = piece[...].astype(F32).reshape(16, 8, 128)
        extended[pl.ds(32 + (2 * axis + up) * 16, 16)] = jnp.where(real, value, zeros)
        reached.add((axis, phase))
    for axis in range(3):
        if (axis, 0) not in reached:
            extended[pl.ds(32 + axis * 32, 32)] = jnp.zeros((32, 8, 128), F32)
        elif (axis, 1) not in reached:
            up, _ = partner(axis, 1, 2)
            extended[pl.ds(32 + (2 * axis + up) * 16, 16)] = zeros


def dot_t(left, right):
    return lax.dot_general(left, right, (((1,), (1,)), ((), ())), preferred_element_type=F32)


def coupled(block, extended, off, columns, first=()):
    vectors = [pair[0] for pair in first] + [extended[columns[k, block]] for k in range(9)]
    matrices = [pair[1] for pair in first] + [off[block, k] for k in range(9)]
    return dot_t(jnp.concatenate(vectors, axis=1).astype(BF16), jnp.concatenate(matrices, axis=1))


def solved(blocks, vectors, factor, straight, crossed):
    matrices = [factor[b] for b in blocks]
    firsts = [dot_t(v.astype(BF16), m) for v, m in zip(vectors, matrices)]
    even = lax.broadcasted_iota(jnp.int32, (8, 128), 1) % 2 == 0
    middles = []
    for b, first in zip(blocks, firsts):
        other = jnp.where(even, pltpu.roll(first, 127, 1), pltpu.roll(first, 1, 1))
        row = pl.ds(b, 1)
        middles.append((straight[row, :] * first + crossed[row, :] * other).astype(BF16))
    return [jnp.dot(v, m, preferred_element_type=F32) for v, m in zip(middles, matrices)]


def for_colour(colour, tables, size, body):
    def step(group, carry):
        body([tables[colour, group * size + j] for j in range(size)])
        return carry

    lax.fori_loop(0, (tables[4, colour] + size - 1) // size, step, 0)


def first_kernel(swaps, q_hbm, faces_hbm, q, faces, *refs):
    sent, sems = refs[:-1], refs[-1]
    copies = [
        pltpu.make_async_copy(faces_hbm, faces, sems.at[0]),
        pltpu.make_async_copy(q_hbm, q, sems.at[1]),
    ]
    for copy in copies:
        copy.start()
    for copy in copies:
        copy.wait()
    send_faces(swaps, q, faces, sent)


def setup_kernel(
    off_hbm, columns_hbm, colours_hbm, diag_ref, off_ref, pairs_ref, off, columns, tables, straight, crossed, colours, sems
):
    half = off_hbm.shape[0] // 2
    loads = [
        pltpu.make_async_copy(colours_hbm, colours, sems.at[0]),
        pltpu.make_async_copy(columns_hbm, columns, sems.at[1]),
        pltpu.make_async_copy(off_hbm.at[pl.ds(0, half)], off.at[pl.ds(0, half)], sems.at[2]),
    ]
    for load in loads:
        load.start()
    pair = lax.broadcasted_iota(jnp.int32, (64, 128), 0)
    lane = lax.broadcasted_iota(jnp.int32, (64, 128), 1)
    spread = jnp.where(lane // 2 == pair, 1.0, 0.0).astype(F32)
    cross = jnp.dot(off_ref[...], spread, precision=lax.Precision.HIGHEST, preferred_element_type=F32)
    paired = jnp.dot(pairs_ref[...].astype(F32), spread, precision=lax.Precision.HIGHEST, preferred_element_type=F32)
    own = diag_ref[...]
    even = lax.broadcasted_iota(jnp.int32, own.shape, 1) % 2 == 0
    other = jnp.where(even, pltpu.roll(own, 127, 1), pltpu.roll(own, 1, 1))
    det = own * other - cross * cross
    straight[...] = jnp.where(paired > 0.5, other / det, 1.0 / own)
    crossed[...] = jnp.where(paired > 0.5, -cross / det, 0.0)
    loads[0].wait()
    for colour in range(4):
        count = jnp.int32(0)
        for block in range(32):
            tables[colour, count] = block
            count = count + jnp.where(colours[block] == colour, 1, 0)
        last = tables[colour, jnp.maximum(count - 1, 0)]
        for j in range(16):
            tables[colour, count + j] = last
        tables[4, colour] = count
    for load in loads[1:]:
        load.wait()


def image_kernel(swaps, tiles, q, diag, off_hbm, off_in, columns, *refs):
    n = len(swaps)
    arrived, (off, image, partial, extended, sems) = refs[:n], refs[n:]
    half, part = off_hbm.shape[0] // 2, 4
    loads = []
    for index in range(half // part):
        rows = pl.ds(half + index * part, part)
        loads.append(pltpu.make_async_copy(off_hbm.at[rows], off.at[rows], sems.at[index]))
        loads[-1].start()
    extend(swaps, q, arrived, extended)

    def step(group, total):
        blocks = [group * part + j for j in range(part)]
        values = [coupled(b, extended, off, columns, [(extended[b], diag[b])]) for b in blocks]
        for b, value in zip(blocks, values):
            image[b] = value
            total = total + q[b] * value
        return total

    total = lax.fori_loop(0, half // part, step, jnp.zeros((8, 128), F32))
    for index, load in enumerate(loads):
        load.wait()
        total = step(half // part + index, total)
    for tile in range(tiles):
        partial[tile] = total


def column_of(values):
    row = lax.broadcasted_iota(jnp.int32, (8, 128), 0)
    out = jnp.zeros((8, 128), F32)
    for n in range(8):
        out = jnp.where(row == n, values[n], out)
    return out


def start_kernel(
    swaps, count, sums, r_ref, image, rho, factor, straight, crossed, tables, faces, r_new, w, norm, alpha, *sent
):
    sigma = jnp.sum(jnp.sum(sums[...], axis=0), axis=1, keepdims=True) / count
    sigma = jnp.where(sigma >= 0, jnp.maximum(sigma, 0.5), jnp.minimum(sigma, -0.5))
    step_size = column_of(rho) / sigma
    alpha[...] = step_size
    new = r_ref[...] - step_size[None] * image[...]
    r_new[...] = new
    norm[...] = jnp.sum(new * new, axis=0)
    w[...] = jnp.zeros_like(w)

    def body(blocks):
        for b, value in zip(blocks, solved(blocks, [r_new[b] for b in blocks], factor, straight, crossed)):
            w[b] = value

    for_colour(0, tables, SOLVE, body)
    send_faces(swaps, w, faces, sent)


def forward_kernel(swaps, colour, r_new, w_in, off, factor, straight, crossed, columns, tables, faces, *refs):
    n = len(swaps)
    arrived, w, sent, (extended, rest) = refs[:n], refs[n], refs[n + 1 : -2], refs[-2:]
    w[...] = w_in[...]
    extend(swaps, w_in, arrived, extended)

    def couple(blocks):
        for b, value in zip(blocks, [coupled(b, extended, off, columns) for b in blocks]):
            rest[b] = r_new[b] - value

    def solve(blocks):
        for b, value in zip(blocks, solved(blocks, [rest[b] for b in blocks], factor, straight, crossed)):
            w[b] = value

    for_colour(colour, tables, COUPLE, couple)
    for_colour(colour, tables, SOLVE, solve)
    if colour == 3:
        z = sent[0]
        z[...] = jnp.zeros_like(z)

        def copy(blocks):
            for b in blocks:
                z[b] = w[b]

        for_colour(3, tables, COUPLE, copy)
        send_faces(swaps, z, faces, sent[1:])
    else:
        send_faces(swaps, w, faces, sent)


def backward_kernel(swaps, tiles, colour, w, z_in, off, factor, straight, crossed, columns, tables, faces, *refs):
    n = len(swaps)
    arrived, others, (extended, rest) = refs[:n], refs[n:-2], refs[-2:]
    if colour == 0:
        r_new, norm, z, partial = others
    else:
        z, sent = others[0], others[1:]
    z[...] = z_in[...]
    extend(swaps, z_in, arrived, extended)

    def couple(blocks):
        for b, value in zip(blocks, [coupled(b, extended, off, columns) for b in blocks]):
            rest[b] = value

    def solve(blocks):
        for b, value in zip(blocks, solved(blocks, [rest[b] for b in blocks], factor, straight, crossed)):
            z[b] = w[b] - value

    for_colour(colour, tables, COUPLE, couple)
    for_colour(colour, tables, SOLVE, solve)
    if colour == 0:
        rho = jnp.sum(r_new[...] * z[...], axis=0)
        both = jnp.concatenate([rho, norm[...]], axis=0)
        for tile in range(tiles):
            partial[tile] = both
    else:
        send_faces(swaps, z, faces, sent)


def last_kernel(count, sums, z, q_ref, x_ref, d_ref, alpha, rho, tau, theta_in, x_new, q_new, d_new, scalars):
    both = jnp.sum(jnp.sum(sums[...], axis=0), axis=1, keepdims=True) / count
    rho_new = both[:8] + jnp.zeros((8, 128), F32)
    norm = both[8:]
    tau_old = column_of(tau)
    theta_old = column_of(theta_in)
    theta = jnp.sqrt(norm + 1e-06) / tau_old
    csq = 1.0 / (1.0 + theta * theta)
    tau_new = tau_old * theta * jnp.sqrt(csq)
    beta = rho_new / column_of(rho)
    q_old = q_ref[...]
    d = (csq * theta_old * theta_old)[None] * d_ref[...] + (csq * alpha[...])[None] * q_old
    d_new[...] = d
    x_new[...] = x_ref[...] + d
    q_new[...] = z[...] + beta[None] * q_old
    row = lax.broadcasted_iota(jnp.int32, (8, 128), 0)
    lane = lax.broadcasted_iota(jnp.int32, (8, 128), 1)
    for index, value in enumerate((rho_new, tau_new, theta)):
        line = jnp.sum(jnp.where(row == lane, value, 0.0), axis=0, keepdims=True)
        scalars[pl.ds(index, 1), :] = line[:, :8]


def vec(*shape, dtype=F32):
    return jax.ShapeDtypeStruct(shape, dtype)


def call(body, outs, places, scratch=(), cost=0, aliases=None):
    return pl.pallas_call(
        body,
        out_shape=outs,
        in_specs=[pl.BlockSpec(memory_space=place) for place in places],
        out_specs=[pl.BlockSpec(memory_space=getattr(out, "memory_space", VMEM)) for out in outs],
        scratch_shapes=list(scratch),
        input_output_aliases=aliases or {},
        cost_estimate=pl.CostEstimate(flops=cost, bytes_accessed=0, transcendentals=0) if cost else None,
        compiler_params=pltpu.CompilerParams(vmem_limit_bytes=8 * 2**20),
    )


def in_hbm(array):
    return pltpu.with_memory_space_constraint(array, HBM)


def per_device(
    x_vec,
    r_vec,
    q_vec,
    d_vec,
    diag_blocks,
    off_blocks,
    columns,
    colours,
    factor_inv,
    pivot_diag,
    pivot_off,
    pivot_pairs,
    face_lists,
    rho_prev,
    tau_prev,
    theta_prev,
):
    tiles = lax.axis_size("gx")
    swaps = swaps_of(tiles)
    n = len(swaps)
    count = float(q_vec.shape[0] * q_vec.shape[2] * tiles)
    kept = VMEM((32, 8, 128), F32)
    pieces = [vec(128, 128, dtype=BF16)] * n
    scratch = [VMEM((128, 8, 128), F32), VMEM((32, 8, 128), F32)]
    off_kept = VMEM(off_blocks.shape, BF16)

    def exchange(sent):
        return [lax.ppermute(piece, "gx", swap[-1]) for piece, swap in zip(sent, swaps)]

    q, faces, *sent = call(
        functools.partial(first_kernel, swaps),
        [kept, SMEM((6, 1, 16), jnp.int32)] + pieces,
        [HBM, HBM],
        [pltpu.SemaphoreType.DMA((2,))],
        cost=10**10,
    )(in_hbm(q_vec), in_hbm(face_lists.transpose(1, 0, 2)))
    arrived = exchange(sent)
    off, columns, tables, straight, crossed = call(
        setup_kernel,
        [off_kept, SMEM((9, 32), jnp.int32), SMEM((8, 128), jnp.int32), vec(32, 128), vec(32, 128)],
        [HBM, HBM, HBM, VMEM, VMEM, VMEM],
        [SMEM((32,), jnp.int32), pltpu.SemaphoreType.DMA((3,))],
    )(in_hbm(off_blocks), in_hbm(columns.T), in_hbm(colours), pivot_diag, pivot_off, pivot_pairs)
    off, image, partial = call(
        functools.partial(image_kernel, swaps, tiles),
        [off_kept, kept, vec(tiles, 8, 128)],
        [VMEM, VMEM, HBM, VMEM, SMEM] + [VMEM] * n,
        [scratch[0], pltpu.SemaphoreType.DMA((4,))],
        aliases={3: 0},
    )(q, diag_blocks, in_hbm(off_blocks), off, columns, *arrived)
    sums = lax.all_to_all(partial, "gx", 0, 0, tiled=True)
    r_new, w, norm, alpha, *sent = call(
        functools.partial(start_kernel, swaps, count),
        [kept, kept, vec(8, 128), vec(8, 128)] + pieces,
        [VMEM] * 3 + [SMEM] + [VMEM] * 3 + [SMEM] * 2,
    )(sums, r_vec, image, rho_prev, factor_inv, straight, crossed, tables, faces)
    fixed = (off, factor_inv, straight, crossed, columns, tables, faces)
    fixed_places = [VMEM] * 4 + [SMEM] * 3
    for colour in (1, 2, 3):
        w, *sent = call(
            functools.partial(forward_kernel, swaps, colour),
            [kept] * (2 if colour == 3 else 1) + pieces,
            [VMEM] * 2 + fixed_places + [VMEM] * n,
            scratch,
        )(r_new, w, *fixed, *exchange(sent))
    z, *sent = sent
    for colour in (2, 1):
        z, *sent = call(
            functools.partial(backward_kernel, swaps, tiles, colour),
            [kept] + pieces,
            [VMEM] * 2 + fixed_places + [VMEM] * n,
            scratch,
        )(w, z, *fixed, *exchange(sent))
    z, partial = call(
        functools.partial(backward_kernel, swaps, tiles, 0),
        [kept, vec(tiles, 16, 128)],
        [VMEM] * 2 + fixed_places + [VMEM] * (n + 2),
        scratch,
    )(w, z, *fixed, *exchange(sent), r_new, norm)
    sums = lax.all_to_all(partial, "gx", 0, 0, tiled=True)
    block_vec = vec(32, 8, 128)
    x_new, q_new, d_new, scalars = call(
        functools.partial(last_kernel, count),
        [block_vec] * 3 + [vec(3, 8)],
        [VMEM] * 6 + [SMEM] * 3,
    )(sums, z, q, x_vec, d_vec, alpha, rho_prev, tau_prev, theta_prev)
    return (x_new, r_new, q_new, d_new, scalars)


def solution(mesh):
    blocks = P(("groups", "gx"))
    return jax.shard_map(
        per_device,
        mesh=mesh,
        in_specs=(blocks,) * 13 + (P("groups"),) * 3,
        out_specs=(blocks,) * 4 + (P(None, "groups"),),
        check_vma=False,
    )
```

```python
import functools

import jax
import jax.numpy as jnp
from jax import lax
from jax.experimental import pallas as pl
from jax.experimental.pallas import tpu as pltpu
from jax.sharding import PartitionSpec as P

F32 = jnp.float32
BF16 = jnp.bfloat16
VMEM = pltpu.VMEM
SMEM = pltpu.SMEM
HBM = pltpu.HBM
SIDE = 4
COUPLE = 4
SOLVE = 16


def swap_pairs(axis, stride, extent, phase, tiles):
    pairs = []
    for tile in range(tiles):
        place = tile // stride % extent
        up = place % 2 == phase
        other = place + 1 if up else place - 1
        if 0 <= other < extent:
            pairs.append((tile, tile + (other - place) * stride))
        elif axis == 0:
            pairs.append((tile, tile + (extent - 1 - 2 * place) * stride))
        else:
            pairs.append((tile, tile ^ 1))
    return pairs


def swaps_of(tiles):
    swaps = []
    for axis, (stride, extent) in enumerate(((1, SIDE), (SIDE, SIDE), (16, tiles // 16))):
        for phase in range(2 if extent > 2 else extent - 1):
            swaps.append((axis, phase, extent, swap_pairs(axis, stride, extent, phase, tiles)))
    return swaps


def partner(axis, phase, extent):
    place = lax.rem(lax.axis_index("gx") // (1, SIDE, 16)[axis], extent)
    up = jnp.where(lax.rem(place, 2) == phase, 1, 0)
    other = place + 2 * up - 1
    return up, (other >= 0) & (other < extent)


def send_faces(swaps, state, faces, sent):
    for (axis, phase, extent, _), out in zip(swaps, sent):
        up, _ = partner(axis, phase, extent)
        face = 2 * axis + 1 - up
        for slot in range(0, 16, 2):
            two = [state[faces[face, 0, slot + j]] for j in range(2)]
            out[pl.ds(slot * 8, 16), :] = jnp.concatenate(two, axis=0).astype(BF16)


def extend(swaps, state, arrived, extended):
    extended[pl.ds(0, 32)] = state[...].astype(BF16).astype(F32)
    zeros = jnp.zeros((16, 8, 128), F32)
    reached = set()
    for (axis, phase, extent, _), piece in zip(swaps, arrived):
        up, real = partner(axis, phase, extent)
        value = piece[pl.ds(0, 128), :].astype(F32).reshape(16, 8, 128)
        extended[pl.ds(32 + (2 * axis + up) * 16, 16)] = jnp.where(real, value, zeros)
        reached.add((axis, phase))
    for axis in range(3):
        if (axis, 0) not in reached:
            extended[pl.ds(32 + axis * 32, 32)] = jnp.zeros((32, 8, 128), F32)
        elif (axis, 1) not in reached:
            up, _ = partner(axis, 1, 2)
            extended[pl.ds(32 + (2 * axis + up) * 16, 16)] = zeros


def dot_t(left, right):
    return lax.dot_general(left, right, (((1,), (1,)), ((), ())), preferred_element_type=F32)


def coupled(block, extended, off, columns, first=()):
    vectors = [pair[0] for pair in first] + [extended[columns[k, block]] for k in range(9)]
    matrices = [pair[1] for pair in first] + [off[block, k] for k in range(9)]
    return dot_t(jnp.concatenate(vectors, axis=1).astype(BF16), jnp.concatenate(matrices, axis=1))


def solved(blocks, vectors, factor, straight, crossed):
    matrices = [factor[b] for b in blocks]
    firsts = [dot_t(v.astype(BF16), m) for v, m in zip(vectors, matrices)]
    even = lax.broadcasted_iota(jnp.int32, (8, 128), 1) % 2 == 0
    middles = []
    for b, first in zip(blocks, firsts):
        other = jnp.where(even, pltpu.roll(first, 127, 1), pltpu.roll(first, 1, 1))
        row = pl.ds(b, 1)
        middles.append((straight[row, :] * first + crossed[row, :] * other).astype(BF16))
    return [jnp.dot(v, m, preferred_element_type=F32) for v, m in zip(middles, matrices)]


def for_colour(colour, tables, size, body):
    def step(group, carry):
        body([tables[colour, group * size + j] for j in range(size)])
        return carry

    lax.fori_loop(0, (tables[4, colour] + size - 1) // size, step, 0)


def first_kernel(swaps, q_hbm, faces_hbm, q, faces, *refs):
    sent, sems = refs[:-1], refs[-1]
    copies = [
        pltpu.make_async_copy(faces_hbm, faces, sems.at[0]),
        pltpu.make_async_copy(q_hbm, q, sems.at[1]),
    ]
    for copy in copies:
        copy.start()
    for copy in copies:
        copy.wait()
    send_faces(swaps, q, faces, sent)


def setup_kernel(
    off_hbm, columns_hbm, colours_hbm, diag_ref, off_ref, pairs_ref, off, columns, tables, straight, crossed, colours, sems
):
    half = off_hbm.shape[0] // 2
    loads = [
        pltpu.make_async_copy(colours_hbm, colours, sems.at[0]),
        pltpu.make_async_copy(columns_hbm, columns, sems.at[1]),
        pltpu.make_async_copy(off_hbm.at[pl.ds(0, half)], off.at[pl.ds(0, half)], sems.at[2]),
    ]
    for load in loads:
        load.start()
    pair = lax.broadcasted_iota(jnp.int32, (64, 128), 0)
    lane = lax.broadcasted_iota(jnp.int32, (64, 128), 1)
    spread = jnp.where(lane // 2 == pair, 1.0, 0.0).astype(F32)
    cross = jnp.dot(off_ref[...], spread, precision=lax.Precision.HIGHEST, preferred_element_type=F32)
    paired = jnp.dot(pairs_ref[...].astype(F32), spread, precision=lax.Precision.HIGHEST, preferred_element_type=F32)
    own = diag_ref[...]
    even = lax.broadcasted_iota(jnp.int32, own.shape, 1) % 2 == 0
    other = jnp.where(even, pltpu.roll(own, 127, 1), pltpu.roll(own, 1, 1))
    det = own * other - cross * cross
    straight[...] = jnp.where(paired > 0.5, other / det, 1.0 / own)
    crossed[...] = jnp.where(paired > 0.5, -cross / det, 0.0)
    loads[0].wait()
    for colour in range(4):
        count = jnp.int32(0)
        for block in range(32):
            tables[colour, count] = block
            count = count + jnp.where(colours[block] == colour, 1, 0)
        last = tables[colour, jnp.maximum(count - 1, 0)]
        for j in range(16):
            tables[colour, count + j] = last
        tables[4, colour] = count
    for load in loads[1:]:
        load.wait()


def image_kernel(swaps, tiles, q, diag, off_hbm, off_in, columns, *refs):
    n = len(swaps)
    arrived, (off, image, partial, extended, sems) = refs[:n], refs[n:]
    half, part = off_hbm.shape[0] // 2, 4
    loads = []
    for index in range(half // part):
        rows = pl.ds(half + index * part, part)
        loads.append(pltpu.make_async_copy(off_hbm.at[rows], off.at[rows], sems.at[index]))
        loads[-1].start()
    extend(swaps, q, arrived, extended)

    def step(group, total):
        blocks = [group * part + j for j in range(part)]
        values = [coupled(b, extended, off, columns, [(extended[b], diag[b])]) for b in blocks]
        for b, value in zip(blocks, values):
            image[b] = value
            total = total + q[b] * value
        return total

    total = lax.fori_loop(0, half // part, step, jnp.zeros((8, 128), F32))
    for index, load in enumerate(loads):
        load.wait()
        total = step(half // part + index, total)
    for tile in range(tiles):
        partial[tile] = total


def column_of(values):
    row = lax.broadcasted_iota(jnp.int32, (8, 128), 0)
    out = jnp.zeros((8, 128), F32)
    for n in range(8):
        out = jnp.where(row == n, values[n], out)
    return out


def start_kernel(
    swaps, count, sums, r_ref, image, rho, factor, straight, crossed, tables, faces, r_new, w, alpha, *sent
):
    sigma = jnp.sum(jnp.sum(sums[...], axis=0), axis=1, keepdims=True) / count
    sigma = jnp.where(sigma >= 0, jnp.maximum(sigma, 0.5), jnp.minimum(sigma, -0.5))
    step_size = column_of(rho) / sigma
    alpha[...] = step_size
    new = r_ref[...] - step_size[None] * image[...]
    r_new[...] = new
    w[...] = jnp.zeros_like(w)

    def body(blocks):
        for b, value in zip(blocks, solved(blocks, [r_new[b] for b in blocks], factor, straight, crossed)):
            w[b] = value

    for_colour(0, tables, SOLVE, body)
    send_faces(swaps, w, faces, sent)


def adjoint_kernel(r_new, w, off, columns, tables, adjoint, terms):
    new = r_new[...]
    terms[pl.ds(0, 8), :] = jnp.sum(new * w[...], axis=0)
    terms[pl.ds(8, 8), :] = jnp.sum(new * new, axis=0)
    adjoint[...] = jnp.zeros_like(adjoint)
    count = tables[4, 0]

    def step(group, carry):
        products = []
        for j in range(COUPLE):
            place = group * COUPLE + j
            block = tables[0, place]
            vector = jnp.where(place < count, w[block], 0.0)
            high = vector.astype(BF16)
            low = (vector - high.astype(F32)).astype(BF16)
            matrix = jnp.concatenate([off[block, k] for k in range(9)], axis=1)
            both = jnp.dot(jnp.concatenate([high, low], axis=0), matrix, preferred_element_type=F32)
            products.append((block, both[:8] + both[8:]))
        for block, product in products:
            for k in range(9):
                column = columns[k, block]
                adjoint[column] = adjoint[column] + product[:, k * 128 : k * 128 + 128]
        return carry

    lax.fori_loop(0, (count + COUPLE - 1) // COUPLE, step, 0)


def gather_kernel(swaps, adjoint, faces, *refs):
    arrived, total = refs[:-1], refs[-1]
    total[...] = adjoint[pl.ds(0, 32)]
    for (axis, phase, extent, _), piece in zip(swaps, arrived):
        up, real = partner(axis, phase, extent)
        face = 2 * axis + 1 - up
        value = piece[pl.ds(128, 128), :].astype(F32).reshape(16, 8, 128)
        value = jnp.where(real, value, 0.0)
        for slot in range(16):
            block = faces[face, 0, slot]
            total[block] = total[block] + value[slot]


def forward_kernel(swaps, colour, r_new, w_in, off, factor, straight, crossed, columns, tables, faces, *refs):
    n = len(swaps)
    arrived, others, (extended, rest) = refs[:n], refs[n:-2], refs[-2:]
    if colour == 1:
        adjoint, others = others[0], others[1:]
    w, sent = others[0], others[1:]
    w[...] = w_in[...]
    extend(swaps, w_in, arrived, extended)

    def couple(blocks):
        for b, value in zip(blocks, [coupled(b, extended, off, columns) for b in blocks]):
            rest[b] = r_new[b] - value

    def solve(blocks):
        for b, value in zip(blocks, solved(blocks, [rest[b] for b in blocks], factor, straight, crossed)):
            w[b] = value

    for_colour(colour, tables, COUPLE, couple)
    for_colour(colour, tables, SOLVE, solve)
    if colour == 3:
        z = sent[0]
        z[...] = jnp.zeros_like(z)

        def copy(blocks):
            for b in blocks:
                z[b] = w[b]

        for_colour(3, tables, COUPLE, copy)
        send_faces(swaps, z, faces, sent[1:])
    else:
        send_faces(swaps, w, faces, sent)
    if colour == 1:
        for (axis, phase, extent, _), out in zip(swaps, sent):
            up, _ = partner(axis, phase, extent)
            value = adjoint[pl.ds(32 + (2 * axis + up) * 16, 16)]
            out[pl.ds(128, 128), :] = value.reshape(128, 128).astype(BF16)


def backward_kernel(swaps, tiles, colour, w, z_in, off, factor, straight, crossed, columns, tables, faces, *refs):
    n = len(swaps)
    arrived, others, (extended, rest) = refs[:n], refs[n:-2], refs[-2:]
    if colour == 1:
        r_new, total, terms, partial = others[0], others[1], others[2], others[-1]
        others = others[3:-1]
    z, sent = others[0], others[1:]
    z[...] = z_in[...]
    extend(swaps, z_in, arrived, extended)

    def couple(blocks):
        for b, value in zip(blocks, [coupled(b, extended, off, columns) for b in blocks]):
            rest[b] = value

    def solve(blocks):
        for b, value in zip(blocks, solved(blocks, [rest[b] for b in blocks], factor, straight, crossed)):
            z[b] = w[b] - value

    for_colour(colour, tables, COUPLE, couple)
    for_colour(colour, tables, SOLVE, solve)
    if colour == 1:
        new = z[...]
        rho = terms[pl.ds(0, 8), :] + jnp.sum(r_new[...] * new - total[...] * new.astype(BF16).astype(F32), axis=0)
        both = jnp.concatenate([rho, terms[pl.ds(8, 8), :]], axis=0)
        for tile in range(tiles):
            partial[tile] = both
    if colour > 0:
        send_faces(swaps, z, faces, sent)


def last_kernel(count, sums, z, q_ref, x_ref, d_ref, alpha, rho, tau, theta_in, x_new, q_new, d_new, scalars):
    both = jnp.sum(jnp.sum(sums[...], axis=0), axis=1, keepdims=True) / count
    rho_new = both[:8] + jnp.zeros((8, 128), F32)
    norm = both[8:]
    tau_old = column_of(tau)
    theta_old = column_of(theta_in)
    theta = jnp.sqrt(norm + 1e-06) / tau_old
    csq = 1.0 / (1.0 + theta * theta)
    tau_new = tau_old * theta * jnp.sqrt(csq)
    beta = rho_new / column_of(rho)
    q_old = q_ref[...]
    d = (csq * theta_old * theta_old)[None] * d_ref[...] + (csq * alpha[...])[None] * q_old
    d_new[...] = d
    x_new[...] = x_ref[...] + d
    q_new[...] = z[...] + beta[None] * q_old
    row = lax.broadcasted_iota(jnp.int32, (8, 128), 0)
    lane = lax.broadcasted_iota(jnp.int32, (8, 128), 1)
    for index, value in enumerate((rho_new, tau_new, theta)):
        line = jnp.sum(jnp.where(row == lane, value, 0.0), axis=0, keepdims=True)
        scalars[pl.ds(index, 1), :] = line[:, :8]


def vec(*shape, dtype=F32):
    return jax.ShapeDtypeStruct(shape, dtype)


def call(body, outs, places, scratch=(), cost=0, aliases=None):
    return pl.pallas_call(
        body,
        out_shape=outs,
        in_specs=[pl.BlockSpec(memory_space=place) for place in places],
        out_specs=[pl.BlockSpec(memory_space=getattr(out, "memory_space", VMEM)) for out in outs],
        scratch_shapes=list(scratch),
        input_output_aliases=aliases or {},
        cost_estimate=pl.CostEstimate(flops=cost, bytes_accessed=0, transcendentals=0) if cost else None,
        compiler_params=pltpu.CompilerParams(vmem_limit_bytes=8 * 2**20),
    )


def in_hbm(array):
    return pltpu.with_memory_space_constraint(array, HBM)


def per_device(
    x_vec,
    r_vec,
    q_vec,
    d_vec,
    diag_blocks,
    off_blocks,
    columns,
    colours,
    factor_inv,
    pivot_diag,
    pivot_off,
    pivot_pairs,
    face_lists,
    rho_prev,
    tau_prev,
    theta_prev,
):
    tiles = lax.axis_size("gx")
    swaps = swaps_of(tiles)
    n = len(swaps)
    count = float(q_vec.shape[0] * q_vec.shape[2] * tiles)
    kept = VMEM((32, 8, 128), F32)
    pieces = [vec(128, 128, dtype=BF16)] * n
    scratch = [VMEM((128, 8, 128), F32), VMEM((32, 8, 128), F32)]
    off_kept = VMEM(off_blocks.shape, BF16)

    def exchange(sent):
        return [lax.ppermute(piece, "gx", swap[-1]) for piece, swap in zip(sent, swaps)]

    q, faces, *sent = call(
        functools.partial(first_kernel, swaps),
        [kept, SMEM((6, 1, 16), jnp.int32)] + pieces,
        [HBM, HBM],
        [pltpu.SemaphoreType.DMA((2,))],
        cost=10**10,
    )(in_hbm(q_vec), in_hbm(face_lists.transpose(1, 0, 2)))
    arrived = exchange(sent)
    off, columns, tables, straight, crossed = call(
        setup_kernel,
        [off_kept, SMEM((9, 32), jnp.int32), SMEM((8, 128), jnp.int32), vec(32, 128), vec(32, 128)],
        [HBM, HBM, HBM, VMEM, VMEM, VMEM],
        [SMEM((32,), jnp.int32), pltpu.SemaphoreType.DMA((3,))],
    )(in_hbm(off_blocks), in_hbm(columns.T), in_hbm(colours), pivot_diag, pivot_off, pivot_pairs)
    off, image, partial = call(
        functools.partial(image_kernel, swaps, tiles),
        [off_kept, kept, vec(tiles, 8, 128)],
        [VMEM, VMEM, HBM, VMEM, SMEM] + [VMEM] * n,
        [scratch[0], pltpu.SemaphoreType.DMA((4,))],
        aliases={3: 0},
    )(q, diag_blocks, in_hbm(off_blocks), off, columns, *arrived)
    sums = lax.all_to_all(partial, "gx", 0, 0, tiled=True)
    r_new, w, alpha, *sent = call(
        functools.partial(start_kernel, swaps, count),
        [kept, kept, vec(8, 128)] + pieces,
        [VMEM] * 3 + [SMEM] + [VMEM] * 3 + [SMEM] * 2,
    )(sums, r_vec, image, rho_prev, factor_inv, straight, crossed, tables, faces)
    fixed = (off, factor_inv, straight, crossed, columns, tables, faces)
    fixed_places = [VMEM] * 4 + [SMEM] * 3
    adjoint, terms = call(
        adjoint_kernel,
        [VMEM((128, 8, 128), F32), VMEM((16, 128), F32)],
        [VMEM] * 3 + [SMEM] * 2,
        cost=10**8,
    )(r_new, w, off, columns, tables)
    for colour in (1, 2, 3):
        arrived = exchange(sent)
        if colour == 2:
            total = call(functools.partial(gather_kernel, swaps), [kept], [VMEM, SMEM] + [VMEM] * n, cost=10**8)(
                adjoint, faces, *arrived
            )[0]
        w, *sent = call(
            functools.partial(forward_kernel, swaps, colour),
            [kept] * (2 if colour == 3 else 1) + ([vec(256, 128, dtype=BF16)] * n if colour == 1 else pieces),
            [VMEM] * 2 + fixed_places + [VMEM] * (n + 1 if colour == 1 else n),
            scratch,
        )(r_new, w, *fixed, *arrived, *([adjoint] if colour == 1 else []))
    z, *sent = sent
    z, *sent = call(
        functools.partial(backward_kernel, swaps, tiles, 2),
        [kept] + pieces,
        [VMEM] * 2 + fixed_places + [VMEM] * n,
        scratch,
    )(w, z, *fixed, *exchange(sent))
    z, *sent, partial = call(
        functools.partial(backward_kernel, swaps, tiles, 1),
        [kept] + pieces + [vec(tiles, 16, 128)],
        [VMEM] * 2 + fixed_places + [VMEM] * (n + 3),
        scratch,
    )(w, z, *fixed, *exchange(sent), r_new, total, terms)
    sums = lax.all_to_all(partial, "gx", 0, 0, tiled=True)
    z = call(
        functools.partial(backward_kernel, swaps, tiles, 0),
        [kept],
        [VMEM] * 2 + fixed_places + [VMEM] * n,
        scratch,
        cost=10**9,
    )(w, z, *fixed, *exchange(sent))[0]
    block_vec = vec(32, 8, 128)
    x_new, q_new, d_new, scalars = call(
        functools.partial(last_kernel, count),
        [block_vec] * 3 + [vec(3, 8)],
        [VMEM] * 6 + [SMEM] * 3,
    )(sums, z, q, x_vec, d_vec, alpha, rho_prev, tau_prev, theta_prev)
    return (x_new, r_new, q_new, d_new, scalars)


def solution(mesh):
    blocks = P(("groups", "gx"))
    return jax.shard_map(
        per_device,
        mesh=mesh,
        in_specs=(blocks,) * 13 + (P("groups"),) * 3,
        out_specs=(blocks,) * 4 + (P(None, "groups"),),
        check_vma=False,
    )
```

```python
import functools

import jax
import jax.numpy as jnp
from jax import lax
from jax.experimental import pallas as pl
from jax.experimental.pallas import tpu as pltpu
from jax.sharding import PartitionSpec as P

F32 = jnp.float32
BF16 = jnp.bfloat16
VMEM = pltpu.VMEM
SMEM = pltpu.SMEM
HBM = pltpu.HBM
SIDE = 4
ORDER = (1, 2, 3, 0, 4, 5)
COUPLE = 4
SOLVE = 16


def swap_pairs(axis, stride, extent, phase, tiles):
    pairs = []
    for tile in range(tiles):
        place = tile // stride % extent
        up = place % 2 == phase
        other = place + 1 if up else place - 1
        if 0 <= other < extent:
            pairs.append((tile, tile + (other - place) * stride))
        elif axis == 0:
            pairs.append((tile, tile + (extent - 1 - 2 * place) * stride))
        else:
            pairs.append((tile, tile ^ 1))
    return pairs


def swaps_of(tiles):
    swaps = []
    for axis, (stride, extent) in enumerate(((1, SIDE), (SIDE, SIDE), (16, tiles // 16))):
        for phase in range(2 if extent > 2 else extent - 1):
            swaps.append((axis, phase, extent, swap_pairs(axis, stride, extent, phase, tiles)))
    return [swaps[i] for i in ORDER if i < len(swaps)]


def partner(axis, phase, extent):
    place = lax.rem(lax.axis_index("gx") // (1, SIDE, 16)[axis], extent)
    up = jnp.where(lax.rem(place, 2) == phase, 1, 0)
    other = place + 2 * up - 1
    return up, (other >= 0) & (other < extent)


def send_faces(swaps, state, faces, sent):
    for (axis, phase, extent, _), out in zip(swaps, sent):
        up, _ = partner(axis, phase, extent)
        face = 2 * axis + 1 - up
        for slot in range(0, 16, 2):
            two = [state[faces[face, 0, slot + j]] for j in range(2)]
            out[pl.ds(slot * 8, 16), :] = jnp.concatenate(two, axis=0).astype(BF16)


def extend(swaps, state, arrived, extended):
    extended[pl.ds(0, 32)] = state[...].astype(BF16).astype(F32)
    zeros = jnp.zeros((16, 8, 128), F32)
    reached = set()
    for (axis, phase, extent, _), piece in zip(swaps, arrived):
        up, real = partner(axis, phase, extent)
        value = piece[pl.ds(0, 128), :].astype(F32).reshape(16, 8, 128)
        extended[pl.ds(32 + (2 * axis + up) * 16, 16)] = jnp.where(real, value, zeros)
        reached.add((axis, phase))
    for axis in range(3):
        if (axis, 0) not in reached:
            extended[pl.ds(32 + axis * 32, 32)] = jnp.zeros((32, 8, 128), F32)
        elif (axis, 1) not in reached:
            up, _ = partner(axis, 1, 2)
            extended[pl.ds(32 + (2 * axis + up) * 16, 16)] = zeros


def dot_t(left, right):
    return lax.dot_general(left, right, (((1,), (1,)), ((), ())), preferred_element_type=F32)


def coupled(block, extended, off, columns, first=()):
    vectors = [pair[0] for pair in first] + [extended[columns[k, block]] for k in range(9)]
    matrices = [pair[1] for pair in first] + [off[block, k] for k in range(9)]
    return dot_t(jnp.concatenate(vectors, axis=1).astype(BF16), jnp.concatenate(matrices, axis=1))


def solved(blocks, vectors, factor, straight, crossed):
    matrices = [factor[b] for b in blocks]
    firsts = [dot_t(v.astype(BF16), m) for v, m in zip(vectors, matrices)]
    even = lax.broadcasted_iota(jnp.int32, (8, 128), 1) % 2 == 0
    middles = []
    for b, first in zip(blocks, firsts):
        other = jnp.where(even, pltpu.roll(first, 127, 1), pltpu.roll(first, 1, 1))
        row = pl.ds(b, 1)
        middles.append((straight[row, :] * first + crossed[row, :] * other).astype(BF16))
    return [jnp.dot(v, m, preferred_element_type=F32) for v, m in zip(middles, matrices)]


def load_kernel(off_hbm, tables, after, off, sems):
    count = tables[4, 0]

    def copy(place):
        block = tables[0, place]
        return pltpu.make_async_copy(off_hbm.at[block], off.at[block], sems.at[place])

    lax.fori_loop(0, count, lambda place, carry: (copy(place).start(), carry)[1], 0)
    lax.fori_loop(0, count, lambda place, carry: (copy(place).wait(), carry)[1], 0)


def for_colour(colour, tables, size, body):
    def step(group, carry):
        body([tables[colour, group * size + j] for j in range(size)])
        return carry

    lax.fori_loop(0, (tables[4, colour] + size - 1) // size, step, 0)


def first_kernel(swaps, q_hbm, faces_hbm, q, faces, *refs):
    sent, sems = refs[:-1], refs[-1]
    copies = [
        pltpu.make_async_copy(faces_hbm, faces, sems.at[0]),
        pltpu.make_async_copy(q_hbm, q, sems.at[1]),
    ]
    for copy in copies:
        copy.start()
    for copy in copies:
        copy.wait()
    send_faces(swaps, q, faces, sent)


def setup_kernel(
    off_hbm, columns_hbm, colours_hbm, diag_ref, off_ref, pairs_ref, off, columns, tables, straight, crossed, colours, sems
):
    half = off_hbm.shape[0] // 2
    loads = [
        pltpu.make_async_copy(colours_hbm, colours, sems.at[0]),
        pltpu.make_async_copy(columns_hbm, columns, sems.at[1]),
        pltpu.make_async_copy(off_hbm.at[pl.ds(0, half)], off.at[pl.ds(0, half)], sems.at[2]),
    ]
    for load in loads:
        load.start()
    pair = lax.broadcasted_iota(jnp.int32, (64, 128), 0)
    lane = lax.broadcasted_iota(jnp.int32, (64, 128), 1)
    spread = jnp.where(lane // 2 == pair, 1.0, 0.0).astype(F32)
    cross = jnp.dot(off_ref[...], spread, precision=lax.Precision.HIGHEST, preferred_element_type=F32)
    paired = jnp.dot(pairs_ref[...].astype(F32), spread, precision=lax.Precision.HIGHEST, preferred_element_type=F32)
    own = diag_ref[...]
    even = lax.broadcasted_iota(jnp.int32, own.shape, 1) % 2 == 0
    other = jnp.where(even, pltpu.roll(own, 127, 1), pltpu.roll(own, 1, 1))
    det = own * other - cross * cross
    straight[...] = jnp.where(paired > 0.5, other / det, 1.0 / own)
    crossed[...] = jnp.where(paired > 0.5, -cross / det, 0.0)
    loads[0].wait()
    for colour in range(4):
        count = jnp.int32(0)
        for block in range(32):
            tables[colour, count] = block
            count = count + jnp.where(colours[block] == colour, 1, 0)
        last = tables[colour, jnp.maximum(count - 1, 0)]
        for j in range(16):
            tables[colour, count + j] = last
        tables[4, colour] = count
    for load in loads[1:]:
        load.wait()


def image_kernel(swaps, tiles, q, diag, off_hbm, off_in, columns, *refs):
    n = len(swaps)
    arrived, (off, image, partial, extended, sems) = refs[:n], refs[n:]
    half, part = off_hbm.shape[0] // 2, 4
    loads = []
    for index in range(half // part):
        rows = pl.ds(half + index * part, part)
        loads.append(pltpu.make_async_copy(off_hbm.at[rows], off.at[rows], sems.at[index]))
        loads[-1].start()
    extend(swaps, q, arrived, extended)

    def step(group, total):
        blocks = [group * part + j for j in range(part)]
        values = [coupled(b, extended, off, columns, [(extended[b], diag[b])]) for b in blocks]
        for b, value in zip(blocks, values):
            image[b] = value
            total = total + q[b] * value
        return total

    total = lax.fori_loop(0, half // part, step, jnp.zeros((8, 128), F32))
    for index, load in enumerate(loads):
        load.wait()
        total = step(half // part + index, total)
    for tile in range(tiles):
        partial[tile] = total


def column_of(values):
    row = lax.broadcasted_iota(jnp.int32, (8, 128), 0)
    out = jnp.zeros((8, 128), F32)
    for n in range(8):
        out = jnp.where(row == n, values[n], out)
    return out


def start_kernel(
    swaps, count, sums, r_ref, image, rho, factor, straight, crossed, tables, faces, r_new, w, alpha, *sent
):
    sigma = jnp.sum(jnp.sum(sums[...], axis=0), axis=1, keepdims=True) / count
    sigma = jnp.where(sigma >= 0, jnp.maximum(sigma, 0.5), jnp.minimum(sigma, -0.5))
    step_size = column_of(rho) / sigma
    alpha[...] = step_size
    new = r_ref[...] - step_size[None] * image[...]
    r_new[...] = new
    w[...] = jnp.zeros_like(w)

    def body(blocks):
        for b, value in zip(blocks, solved(blocks, [r_new[b] for b in blocks], factor, straight, crossed)):
            w[b] = value

    for_colour(0, tables, SOLVE, body)
    send_faces(swaps, w, faces, sent)


def adjoint_kernel(r_new, w, off, columns, tables, adjoint, terms):
    new = r_new[...]
    terms[pl.ds(0, 8), :] = jnp.sum(new * w[...], axis=0)
    terms[pl.ds(8, 8), :] = jnp.sum(new * new, axis=0)
    adjoint[...] = jnp.zeros_like(adjoint)
    count = tables[4, 0]

    def step(group, carry):
        products = []
        for j in range(COUPLE):
            place = group * COUPLE + j
            block = tables[0, place]
            vector = jnp.where(place < count, w[block], 0.0)
            high = vector.astype(BF16)
            low = (vector - high.astype(F32)).astype(BF16)
            matrix = jnp.concatenate([off[block, k] for k in range(9)], axis=1)
            both = jnp.dot(jnp.concatenate([high, low], axis=0), matrix, preferred_element_type=F32)
            products.append((block, both[:8] + both[8:]))
        for block, product in products:
            for k in range(9):
                column = columns[k, block]
                adjoint[column] = adjoint[column] + product[:, k * 128 : k * 128 + 128]
        return carry

    lax.fori_loop(0, (count + COUPLE - 1) // COUPLE, step, 0)


def gather_kernel(swaps, adjoint, faces, *refs):
    arrived, total = refs[:-1], refs[-1]
    total[...] = adjoint[pl.ds(0, 32)]
    for (axis, phase, extent, _), piece in zip(swaps, arrived):
        up, real = partner(axis, phase, extent)
        face = 2 * axis + 1 - up
        value = piece[pl.ds(128, 128), :].astype(F32).reshape(16, 8, 128)
        value = jnp.where(real, value, 0.0)
        for slot in range(16):
            block = faces[face, 0, slot]
            total[block] = total[block] + value[slot]


def forward_kernel(swaps, colour, r_new, w_in, off, factor, straight, crossed, columns, tables, faces, *refs):
    n = len(swaps)
    arrived, others, (extended, rest) = refs[:n], refs[n:-2], refs[-2:]
    if colour == 1:
        adjoint, others = others[0], others[1:]
    w, sent = others[0], others[1:]
    w[...] = w_in[...]
    extend(swaps, w_in, arrived, extended)

    def couple(blocks):
        for b, value in zip(blocks, [coupled(b, extended, off, columns) for b in blocks]):
            rest[b] = r_new[b] - value

    def solve(blocks):
        for b, value in zip(blocks, solved(blocks, [rest[b] for b in blocks], factor, straight, crossed)):
            w[b] = value

    for_colour(colour, tables, COUPLE, couple)
    for_colour(colour, tables, SOLVE, solve)
    if colour == 3:
        z = sent[0]
        z[...] = jnp.zeros_like(z)

        def copy(blocks):
            for b in blocks:
                z[b] = w[b]

        for_colour(3, tables, COUPLE, copy)
        send_faces(swaps, z, faces, sent[1:])
    else:
        send_faces(swaps, w, faces, sent)
    if colour == 1:
        for (axis, phase, extent, _), out in zip(swaps, sent):
            up, _ = partner(axis, phase, extent)
            value = adjoint[pl.ds(32 + (2 * axis + up) * 16, 16)]
            out[pl.ds(128, 128), :] = value.reshape(128, 128).astype(BF16)


def backward_kernel(swaps, tiles, colour, w, z_in, off, factor, straight, crossed, columns, tables, faces, *refs):
    n = len(swaps)
    arrived, others, (extended, rest) = refs[:n], refs[n:-2], refs[-2:]
    if colour == 1:
        r_new, total, terms, partial = others[0], others[1], others[2], others[-1]
        others = others[3:-1]
    z, sent = others[0], others[1:]
    z[...] = z_in[...]
    extend(swaps, z_in, arrived, extended)

    def couple(blocks):
        for b, value in zip(blocks, [coupled(b, extended, off, columns) for b in blocks]):
            rest[b] = value

    def solve(blocks):
        for b, value in zip(blocks, solved(blocks, [rest[b] for b in blocks], factor, straight, crossed)):
            z[b] = w[b] - value

    for_colour(colour, tables, COUPLE, couple)
    for_colour(colour, tables, SOLVE, solve)
    if colour == 1:
        new = z[...]
        rho = terms[pl.ds(0, 8), :] + jnp.sum(r_new[...] * new - total[...] * new.astype(BF16).astype(F32), axis=0)
        both = jnp.concatenate([rho, terms[pl.ds(8, 8), :]], axis=0)
        for tile in range(tiles):
            partial[tile] = both
    if colour > 0:
        send_faces(swaps, z, faces, sent)


def last_kernel(count, sums, z, q_ref, x_ref, d_ref, alpha, rho, tau, theta_in, x_new, q_new, d_new, scalars):
    both = jnp.sum(jnp.sum(sums[...], axis=0), axis=1, keepdims=True) / count
    rho_new = both[:8] + jnp.zeros((8, 128), F32)
    norm = both[8:]
    tau_old = column_of(tau)
    theta_old = column_of(theta_in)
    theta = jnp.sqrt(norm + 1e-06) / tau_old
    csq = 1.0 / (1.0 + theta * theta)
    tau_new = tau_old * theta * jnp.sqrt(csq)
    beta = rho_new / column_of(rho)
    q_old = q_ref[...]
    d = (csq * theta_old * theta_old)[None] * d_ref[...] + (csq * alpha[...])[None] * q_old
    d_new[...] = d
    x_new[...] = x_ref[...] + d
    q_new[...] = z[...] + beta[None] * q_old
    row = lax.broadcasted_iota(jnp.int32, (8, 128), 0)
    lane = lax.broadcasted_iota(jnp.int32, (8, 128), 1)
    for index, value in enumerate((rho_new, tau_new, theta)):
        line = jnp.sum(jnp.where(row == lane, value, 0.0), axis=0, keepdims=True)
        scalars[pl.ds(index, 1), :] = line[:, :8]


def vec(*shape, dtype=F32):
    return jax.ShapeDtypeStruct(shape, dtype)


def call(body, outs, places, scratch=(), cost=0, aliases=None):
    return pl.pallas_call(
        body,
        out_shape=outs,
        in_specs=[pl.BlockSpec(memory_space=place) for place in places],
        out_specs=[pl.BlockSpec(memory_space=getattr(out, "memory_space", VMEM)) for out in outs],
        scratch_shapes=list(scratch),
        input_output_aliases=aliases or {},
        cost_estimate=pl.CostEstimate(flops=cost, bytes_accessed=0, transcendentals=0) if cost else None,
        compiler_params=pltpu.CompilerParams(vmem_limit_bytes=8 * 2**20),
    )


def in_hbm(array):
    return pltpu.with_memory_space_constraint(array, HBM)


def per_device(
    x_vec,
    r_vec,
    q_vec,
    d_vec,
    diag_blocks,
    off_blocks,
    columns,
    colours,
    factor_inv,
    pivot_diag,
    pivot_off,
    pivot_pairs,
    face_lists,
    rho_prev,
    tau_prev,
    theta_prev,
):
    tiles = lax.axis_size("gx")
    swaps = swaps_of(tiles)
    n = len(swaps)
    count = float(q_vec.shape[0] * q_vec.shape[2] * tiles)
    kept = VMEM((32, 8, 128), F32)
    pieces = [vec(128, 128, dtype=BF16)] * n
    scratch = [VMEM((128, 8, 128), F32), VMEM((32, 8, 128), F32)]
    off_kept = VMEM(off_blocks.shape, BF16)

    def exchange(sent):
        return [lax.ppermute(piece, "gx", swap[-1]) for piece, swap in zip(sent, swaps)]

    q, faces, *sent = call(
        functools.partial(first_kernel, swaps),
        [kept, SMEM((6, 1, 16), jnp.int32)] + pieces,
        [HBM, HBM],
        [pltpu.SemaphoreType.DMA((2,))],
        cost=10**10,
    )(in_hbm(q_vec), in_hbm(face_lists.transpose(1, 0, 2)))
    arrived = exchange(sent)
    off, columns, tables, straight, crossed = call(
        setup_kernel,
        [off_kept, SMEM((9, 32), jnp.int32), SMEM((8, 128), jnp.int32), vec(32, 128), vec(32, 128)],
        [HBM, HBM, HBM, VMEM, VMEM, VMEM],
        [SMEM((32,), jnp.int32), pltpu.SemaphoreType.DMA((3,))],
    )(in_hbm(off_blocks), in_hbm(columns.T), in_hbm(colours), pivot_diag, pivot_off, pivot_pairs)
    off, image, partial = call(
        functools.partial(image_kernel, swaps, tiles),
        [off_kept, kept, vec(tiles, 8, 128)],
        [VMEM, VMEM, HBM, VMEM, SMEM] + [VMEM] * n,
        [scratch[0], pltpu.SemaphoreType.DMA((4,))],
        aliases={3: 0},
    )(q, diag_blocks, in_hbm(off_blocks), off, columns, *arrived)
    sums = lax.all_to_all(partial, "gx", 0, 0, tiled=True)
    r_new, w, alpha, *sent = call(
        functools.partial(start_kernel, swaps, count),
        [kept, kept, vec(8, 128)] + pieces,
        [VMEM] * 3 + [SMEM] + [VMEM] * 3 + [SMEM] * 2,
    )(sums, r_vec, image, rho_prev, factor_inv, straight, crossed, tables, faces)
    fixed = (off, factor_inv, straight, crossed, columns, tables, faces)
    fixed_places = [VMEM] * 4 + [SMEM] * 3
    adjoint, terms = call(
        adjoint_kernel,
        [VMEM((128, 8, 128), F32), VMEM((16, 128), F32)],
        [VMEM] * 3 + [SMEM] * 2,
        cost=10**8,
    )(r_new, w, off, columns, tables)
    for colour in (1, 2, 3):
        arrived = exchange(sent)
        if colour == 2:
            total = call(functools.partial(gather_kernel, swaps), [kept], [VMEM, SMEM] + [VMEM] * n, cost=10**8)(
                adjoint, faces, *arrived
            )[0]
        w, *sent = call(
            functools.partial(forward_kernel, swaps, colour),
            [kept] * (2 if colour == 3 else 1) + ([vec(256, 128, dtype=BF16)] * n if colour == 1 else pieces),
            [VMEM] * 2 + fixed_places + [VMEM] * (n + 1 if colour == 1 else n),
            scratch,
        )(r_new, w, *fixed, *arrived, *([adjoint] if colour == 1 else []))
    z, *sent = sent
    z, *sent = call(
        functools.partial(backward_kernel, swaps, tiles, 2),
        [kept] + pieces,
        [VMEM] * 2 + fixed_places + [VMEM] * n,
        scratch,
    )(w, z, *fixed, *exchange(sent))
    z, *sent, partial = call(
        functools.partial(backward_kernel, swaps, tiles, 1),
        [kept] + pieces + [vec(tiles, 16, 128)],
        [VMEM] * 2 + fixed_places + [VMEM] * (n + 3),
        scratch,
    )(w, z, *fixed, *exchange(sent), r_new, total, terms)
    sums = lax.all_to_all(partial, "gx", 0, 0, tiled=True)
    arrived = exchange(sent)
    off = call(load_kernel, [off_kept], [HBM, SMEM, VMEM], [pltpu.SemaphoreType.DMA((32,))], cost=10**8)(
        in_hbm(off_blocks), tables, arrived[0]
    )[0]
    z = call(
        functools.partial(backward_kernel, swaps, tiles, 0),
        [kept],
        [VMEM] * 2 + fixed_places + [VMEM] * n,
        scratch,
    )(w, z, off, *fixed[1:], *arrived)[0]
    block_vec = vec(32, 8, 128)
    x_new, q_new, d_new, scalars = call(
        functools.partial(last_kernel, count),
        [block_vec] * 3 + [vec(3, 8)],
        [VMEM] * 6 + [SMEM] * 3,
    )(sums, z, q, x_vec, d_vec, alpha, rho_prev, tau_prev, theta_prev)
    return (x_new, r_new, q_new, d_new, scalars)


def solution(mesh):
    blocks = P(("groups", "gx"))
    return jax.shard_map(
        per_device,
        mesh=mesh,
        in_specs=(blocks,) * 13 + (P("groups"),) * 3,
        out_specs=(blocks,) * 4 + (P(None, "groups"),),
        check_vma=False,
    )
```

```python
import functools

import jax
import jax.numpy as jnp
from jax import lax
from jax.experimental import pallas as pl
from jax.experimental.pallas import tpu as pltpu
from jax.sharding import PartitionSpec as P

F32 = jnp.float32
BF16 = jnp.bfloat16
VMEM = pltpu.VMEM
SMEM = pltpu.SMEM
HBM = pltpu.HBM
SIDE = 4
ORDER = (1, 2, 3, 0, 4, 5)
COUPLE = (8, 4)
SOLVE = (16,)
PART = 4
PARTS = (0, 12, 16, 24, 32)


def swap_pairs(axis, stride, extent, phase, tiles):
    pairs = []
    for tile in range(tiles):
        place = tile // stride % extent
        up = place % 2 == phase
        other = place + 1 if up else place - 1
        if 0 <= other < extent:
            pairs.append((tile, tile + (other - place) * stride))
        elif axis == 0:
            pairs.append((tile, tile + (extent - 1 - 2 * place) * stride))
        else:
            pairs.append((tile, tile ^ 1))
    return pairs


def swaps_of(tiles):
    swaps = []
    for axis, (stride, extent) in enumerate(((1, SIDE), (SIDE, SIDE), (16, tiles // 16))):
        for phase in range(2 if extent > 2 else extent - 1):
            swaps.append((axis, phase, extent, swap_pairs(axis, stride, extent, phase, tiles)))
    return [swaps[i] for i in ORDER if i < len(swaps)]


def partner(axis, phase, extent):
    place = lax.rem(lax.axis_index("gx") // (1, SIDE, 16)[axis], extent)
    up = jnp.where(lax.rem(place, 2) == phase, 1, 0)
    other = place + 2 * up - 1
    return up, (other >= 0) & (other < extent)


def send_faces(swaps, state, faces, sent):
    for (axis, phase, extent, _), out in zip(swaps, sent):
        up, _ = partner(axis, phase, extent)
        face = 2 * axis + 1 - up
        for slot in range(0, 16, 2):
            two = [state[faces[face, 0, slot + j]] for j in range(2)]
            out[pl.ds(slot * 8, 16), :] = jnp.concatenate(two, axis=0).astype(BF16)


def extend(swaps, state, arrived, extended):
    extended[pl.ds(0, 32)] = state[...].astype(BF16).astype(F32)
    zeros = jnp.zeros((16, 8, 128), F32)
    reached = set()
    for (axis, phase, extent, _), piece in zip(swaps, arrived):
        up, real = partner(axis, phase, extent)
        value = piece[pl.ds(0, 128), :].astype(F32).reshape(16, 8, 128)
        extended[pl.ds(32 + (2 * axis + up) * 16, 16)] = jnp.where(real, value, zeros)
        reached.add((axis, phase))
    for axis in range(3):
        if (axis, 0) not in reached:
            extended[pl.ds(32 + axis * 32, 32)] = jnp.zeros((32, 8, 128), F32)
        elif (axis, 1) not in reached:
            up, _ = partner(axis, 1, 2)
            extended[pl.ds(32 + (2 * axis + up) * 16, 16)] = zeros


def dot_t(left, right):
    return lax.dot_general(left, right, (((1,), (1,)), ((), ())), preferred_element_type=F32)


def coupled(block, extended, off, columns, first=()):
    vectors = [pair[0] for pair in first] + [extended[columns[k, block]] for k in range(9)]
    matrices = [pair[1] for pair in first] + [off[block, k] for k in range(9)]
    return dot_t(jnp.concatenate(vectors, axis=1).astype(BF16), jnp.concatenate(matrices, axis=1))


def solved(blocks, vectors, factor, straight, crossed):
    matrices = [factor[b] for b in blocks]
    pairs = range(0, len(blocks), 2)
    firsts = []
    for j in pairs:
        both = dot_t(jnp.concatenate(vectors[j : j + 2], axis=0).astype(BF16), jnp.concatenate(matrices[j : j + 2], axis=0))
        firsts += [both[:8, :128], both[8:, 128:]]
    even = lax.broadcasted_iota(jnp.int32, (8, 128), 1) % 2 == 0
    middles = []
    for b, first in zip(blocks, firsts):
        other = jnp.where(even, pltpu.roll(first, 127, 1), pltpu.roll(first, 1, 1))
        row = pl.ds(b, 1)
        middles.append(straight[row, :] * first + crossed[row, :] * other)
    values = []
    for j in pairs:
        left = jnp.concatenate(middles[j : j + 2], axis=0).astype(BF16)
        both = jnp.dot(left, jnp.concatenate(matrices[j : j + 2], axis=1), preferred_element_type=F32)
        values += [both[:8, :128], both[8:, 128:]]
    return values


def load_kernel(off_hbm, tables, after, off, sems):
    count = tables[4, 0]

    def copy(place):
        block = tables[0, place]
        return pltpu.make_async_copy(off_hbm.at[block], off.at[block], sems.at[place])

    lax.fori_loop(0, count, lambda place, carry: (copy(place).start(), carry)[1], 0)
    lax.fori_loop(0, count, lambda place, carry: (copy(place).wait(), carry)[1], 0)


def for_colour(colour, tables, sizes, body):
    count = tables[4, colour]
    done = 0
    for size in sizes:
        left = count - done
        groups = (left + size - 1) // size if size == sizes[-1] else left // size

        def step(group, carry, done=done, size=size):
            body([tables[colour, done + group * size + j] for j in range(size)])
            return carry

        lax.fori_loop(0, groups, step, 0)
        done = done + groups * size


def first_kernel(swaps, q_hbm, faces_hbm, q, faces, *refs):
    sent, sems = refs[:-1], refs[-1]
    copies = [
        pltpu.make_async_copy(faces_hbm, faces, sems.at[0]),
        pltpu.make_async_copy(q_hbm, q, sems.at[1]),
    ]
    for copy in copies:
        copy.start()
    for copy in copies:
        copy.wait()
    send_faces(swaps, q, faces, sent)


def setup_kernel(
    off_hbm, columns_hbm, colours_hbm, diag_ref, off_ref, pairs_ref, off, columns, tables, straight, crossed, colours, sems
):
    loads = [
        pltpu.make_async_copy(colours_hbm, colours, sems.at[0]),
        pltpu.make_async_copy(columns_hbm, columns, sems.at[1]),
        pltpu.make_async_copy(off_hbm.at[pl.ds(0, PARTS[1])], off.at[pl.ds(0, PARTS[1])], sems.at[2]),
    ]
    for load in loads:
        load.start()
    pair = lax.broadcasted_iota(jnp.int32, (64, 128), 0)
    lane = lax.broadcasted_iota(jnp.int32, (64, 128), 1)
    spread = jnp.where(lane // 2 == pair, 1.0, 0.0).astype(F32)
    cross = jnp.dot(off_ref[...], spread, precision=lax.Precision.HIGHEST, preferred_element_type=F32)
    paired = jnp.dot(pairs_ref[...].astype(F32), spread, precision=lax.Precision.HIGHEST, preferred_element_type=F32)
    own = diag_ref[...]
    even = lax.broadcasted_iota(jnp.int32, own.shape, 1) % 2 == 0
    other = jnp.where(even, pltpu.roll(own, 127, 1), pltpu.roll(own, 1, 1))
    det = own * other - cross * cross
    straight[...] = jnp.where(paired > 0.5, other / det, 1.0 / own)
    crossed[...] = jnp.where(paired > 0.5, -cross / det, 0.0)
    loads[0].wait()
    for colour in range(4):
        count = jnp.int32(0)
        for block in range(32):
            tables[colour, count] = block
            count = count + jnp.where(colours[block] == colour, 1, 0)
        last = tables[colour, jnp.maximum(count - 1, 0)]
        for j in range(16):
            tables[colour, count + j] = last
        tables[4, colour] = count
    for load in loads[1:]:
        load.wait()


def image_kernel(swaps, tiles, q, diag, off_hbm, off_in, columns, *refs):
    n = len(swaps)
    arrived, (off, image, partial, extended, sems) = refs[:n], refs[n:]
    loads = [None]
    for start, end in zip(PARTS[1:], PARTS[2:]):
        rows = pl.ds(start, end - start)
        loads.append(pltpu.make_async_copy(off_hbm.at[rows], off.at[rows], sems.at[len(loads) - 1]))
        loads[-1].start()
    extend(swaps, q, arrived, extended)

    total = jnp.zeros((8, 128), F32)
    for load, start, end in zip(loads, PARTS, PARTS[1:]):
        if load is not None:
            load.wait()
        blocks = range(start, end)
        values = [coupled(b, extended, off, columns, [(extended[b], diag[b])]) for b in blocks]
        for b, value in zip(blocks, values):
            image[b] = value
            total = total + q[b] * value
    for tile in range(tiles):
        partial[tile] = total


def column_of(values):
    row = lax.broadcasted_iota(jnp.int32, (8, 128), 0)
    out = jnp.zeros((8, 128), F32)
    for n in range(8):
        out = jnp.where(row == n, values[n], out)
    return out


def start_kernel(
    swaps, count, sums, r_ref, image, rho, factor, straight, crossed, tables, faces, r_new, w, alpha, *sent
):
    sigma = jnp.sum(jnp.sum(sums[...], axis=0), axis=1, keepdims=True) / count
    sigma = jnp.where(sigma >= 0, jnp.maximum(sigma, 0.5), jnp.minimum(sigma, -0.5))
    step_size = column_of(rho) / sigma
    alpha[...] = step_size
    new = r_ref[...] - step_size[None] * image[...]
    r_new[...] = new
    w[...] = jnp.zeros_like(w)

    def body(blocks):
        for b, value in zip(blocks, solved(blocks, [r_new[b] for b in blocks], factor, straight, crossed)):
            w[b] = value

    for_colour(0, tables, SOLVE, body)
    send_faces(swaps, w, faces, sent)


def adjoint_kernel(r_new, w, off, columns, tables, adjoint, terms, r_out):
    new = r_new[...]
    r_out[...] = new
    terms[pl.ds(0, 8), :] = jnp.sum(new * w[...], axis=0)
    terms[pl.ds(8, 8), :] = jnp.sum(new * new, axis=0)
    adjoint[...] = jnp.zeros_like(adjoint)
    count = tables[4, 0]

    def step(group, carry):
        products = []
        for j in range(PART):
            place = group * PART + j
            block = tables[0, place]
            vector = jnp.where(place < count, w[block], 0.0)
            high = vector.astype(BF16)
            low = (vector - high.astype(F32)).astype(BF16)
            matrix = jnp.concatenate([off[block, k] for k in range(9)], axis=1)
            both = jnp.dot(jnp.concatenate([high, low], axis=0), matrix, preferred_element_type=F32)
            products.append((block, both[:8] + both[8:]))
        for block, product in products:
            for k in range(9):
                column = columns[k, block]
                adjoint[column] = adjoint[column] + product[:, k * 128 : k * 128 + 128]
        return carry

    lax.fori_loop(0, (count + PART - 1) // PART, step, 0)


def gather_kernel(swaps, adjoint, faces, *refs):
    arrived, total = refs[:-1], refs[-1]
    total[...] = adjoint[pl.ds(0, 32)]
    for (axis, phase, extent, _), piece in zip(swaps, arrived):
        up, real = partner(axis, phase, extent)
        face = 2 * axis + 1 - up
        value = piece[pl.ds(128, 128), :].astype(F32).reshape(16, 8, 128)
        value = jnp.where(real, value, 0.0)
        for slot in range(16):
            block = faces[face, 0, slot]
            total[block] = total[block] + value[slot]


def forward_kernel(swaps, colour, r_new, w_in, off, factor, straight, crossed, columns, tables, faces, *refs):
    n = len(swaps)
    arrived, others, (extended, rest) = refs[:n], refs[n:-2], refs[-2:]
    if colour == 1:
        adjoint, others = others[0], others[1:]
    w, sent = others[0], others[1:]
    w[...] = w_in[...]
    extend(swaps, w_in, arrived, extended)

    def couple(blocks):
        for b, value in zip(blocks, [coupled(b, extended, off, columns) for b in blocks]):
            rest[b] = r_new[b] - value

    def solve(blocks):
        for b, value in zip(blocks, solved(blocks, [rest[b] for b in blocks], factor, straight, crossed)):
            w[b] = value

    for_colour(colour, tables, COUPLE, couple)
    for_colour(colour, tables, SOLVE, solve)
    if colour == 3:
        z = sent[0]
        z[...] = jnp.zeros_like(z)

        def copy(blocks):
            for b in blocks:
                z[b] = w[b]

        for_colour(3, tables, COUPLE, copy)
        send_faces(swaps, z, faces, sent[1:])
    else:
        send_faces(swaps, w, faces, sent)
    if colour == 1:
        for (axis, phase, extent, _), out in zip(swaps, sent):
            up, _ = partner(axis, phase, extent)
            value = adjoint[pl.ds(32 + (2 * axis + up) * 16, 16)]
            out[pl.ds(128, 128), :] = value.reshape(128, 128).astype(BF16)


def backward_kernel(swaps, tiles, colour, w, z_in, off, factor, straight, crossed, columns, tables, faces, *refs):
    n = len(swaps)
    arrived, others, (extended, rest) = refs[:n], refs[n:-2], refs[-2:]
    if colour == 1:
        r_new, total, terms, partial = others[0], others[1], others[2], others[-1]
        others = others[3:-1]
    z, sent = others[0], others[1:]
    z[...] = z_in[...]
    extend(swaps, z_in, arrived, extended)

    def couple(blocks):
        for b, value in zip(blocks, [coupled(b, extended, off, columns) for b in blocks]):
            rest[b] = value

    def solve(blocks):
        for b, value in zip(blocks, solved(blocks, [rest[b] for b in blocks], factor, straight, crossed)):
            z[b] = w[b] - value

    for_colour(colour, tables, COUPLE, couple)
    for_colour(colour, tables, SOLVE, solve)
    if colour == 1:
        new = z[...]
        rho = terms[pl.ds(0, 8), :] + jnp.sum(r_new[...] * new - total[...] * new.astype(BF16).astype(F32), axis=0)
        both = jnp.concatenate([rho, terms[pl.ds(8, 8), :]], axis=0)
        for tile in range(tiles):
            partial[tile] = both
    if colour > 0:
        send_faces(swaps, z, faces, sent)


def last_kernel(count, sums, z, q_ref, x_ref, d_ref, alpha, rho, tau, theta_in, x_new, q_new, d_new, scalars):
    both = jnp.sum(jnp.sum(sums[...], axis=0), axis=1, keepdims=True) / count
    rho_new = both[:8] + jnp.zeros((8, 128), F32)
    norm = both[8:]
    tau_old = column_of(tau)
    theta_old = column_of(theta_in)
    theta = jnp.sqrt(norm + 1e-06) / tau_old
    csq = 1.0 / (1.0 + theta * theta)
    tau_new = tau_old * theta * jnp.sqrt(csq)
    beta = rho_new / column_of(rho)
    q_old = q_ref[...]
    d = (csq * theta_old * theta_old)[None] * d_ref[...] + (csq * alpha[...])[None] * q_old
    d_new[...] = d
    x_new[...] = x_ref[...] + d
    q_new[...] = z[...] + beta[None] * q_old
    row = lax.broadcasted_iota(jnp.int32, (8, 128), 0)
    lane = lax.broadcasted_iota(jnp.int32, (8, 128), 1)
    for index, value in enumerate((rho_new, tau_new, theta)):
        line = jnp.sum(jnp.where(row == lane, value, 0.0), axis=0, keepdims=True)
        scalars[pl.ds(index, 1), :] = line[:, :8]


def vec(*shape, dtype=F32):
    return jax.ShapeDtypeStruct(shape, dtype)


def call(body, outs, places, scratch=(), cost=0, aliases=None):
    return pl.pallas_call(
        body,
        out_shape=outs,
        in_specs=[pl.BlockSpec(memory_space=place) for place in places],
        out_specs=[pl.BlockSpec(memory_space=getattr(out, "memory_space", VMEM)) for out in outs],
        scratch_shapes=list(scratch),
        input_output_aliases=aliases or {},
        cost_estimate=pl.CostEstimate(flops=cost, bytes_accessed=0, transcendentals=0) if cost else None,
        compiler_params=pltpu.CompilerParams(vmem_limit_bytes=8 * 2**20),
    )


def in_hbm(array):
    return pltpu.with_memory_space_constraint(array, HBM)


def per_device(
    x_vec,
    r_vec,
    q_vec,
    d_vec,
    diag_blocks,
    off_blocks,
    columns,
    colours,
    factor_inv,
    pivot_diag,
    pivot_off,
    pivot_pairs,
    face_lists,
    rho_prev,
    tau_prev,
    theta_prev,
):
    tiles = lax.axis_size("gx")
    swaps = swaps_of(tiles)
    n = len(swaps)
    count = float(q_vec.shape[0] * q_vec.shape[2] * tiles)
    kept = VMEM((32, 8, 128), F32)
    pieces = [vec(128, 128, dtype=BF16)] * n
    scratch = [VMEM((128, 8, 128), F32), VMEM((32, 8, 128), F32)]
    off_kept = VMEM(off_blocks.shape, BF16)

    def exchange(sent):
        return [lax.ppermute(piece, "gx", swap[-1]) for piece, swap in zip(sent, swaps)]

    q, faces, *sent = call(
        functools.partial(first_kernel, swaps),
        [kept, SMEM((6, 1, 16), jnp.int32)] + pieces,
        [HBM, HBM],
        [pltpu.SemaphoreType.DMA((2,))],
        cost=10**10,
    )(in_hbm(q_vec), in_hbm(face_lists.transpose(1, 0, 2)))
    arrived = exchange(sent)
    off, columns, tables, straight, crossed = call(
        setup_kernel,
        [off_kept, SMEM((9, 32), jnp.int32), SMEM((8, 128), jnp.int32), vec(32, 128), vec(32, 128)],
        [HBM, HBM, HBM, VMEM, VMEM, VMEM],
        [SMEM((32,), jnp.int32), pltpu.SemaphoreType.DMA((3,))],
    )(in_hbm(off_blocks), in_hbm(columns.T), in_hbm(colours), pivot_diag, pivot_off, pivot_pairs)
    off, image, partial = call(
        functools.partial(image_kernel, swaps, tiles),
        [off_kept, kept, vec(tiles, 8, 128)],
        [VMEM, VMEM, HBM, VMEM, SMEM] + [VMEM] * n,
        [scratch[0], pltpu.SemaphoreType.DMA((4,))],
        aliases={3: 0},
    )(q, diag_blocks, in_hbm(off_blocks), off, columns, *arrived)
    sums = lax.all_to_all(partial, "gx", 0, 0, tiled=True)
    r_new, w, alpha, *sent = call(
        functools.partial(start_kernel, swaps, count),
        [kept, kept, vec(8, 128)] + pieces,
        [VMEM] * 3 + [SMEM] + [VMEM] * 3 + [SMEM] * 2,
    )(sums, r_vec, image, rho_prev, factor_inv, straight, crossed, tables, faces)
    fixed = (off, factor_inv, straight, crossed, columns, tables, faces)
    fixed_places = [VMEM] * 4 + [SMEM] * 3
    adjoint, terms, r_out = call(
        adjoint_kernel,
        [VMEM((128, 8, 128), F32), VMEM((16, 128), F32), vec(32, 8, 128)],
        [VMEM] * 3 + [SMEM] * 2,
        cost=10**8,
    )(r_new, w, off, columns, tables)
    for colour in (1, 2, 3):
        arrived = exchange(sent)
        if colour == 2:
            total = call(functools.partial(gather_kernel, swaps), [kept], [VMEM, SMEM] + [VMEM] * n, cost=10**8)(
                adjoint, faces, *arrived
            )[0]
        w, *sent = call(
            functools.partial(forward_kernel, swaps, colour),
            [kept] * (2 if colour == 3 else 1) + ([vec(256, 128, dtype=BF16)] * n if colour == 1 else pieces),
            [VMEM] * 2 + fixed_places + [VMEM] * (n + 1 if colour == 1 else n),
            scratch,
        )(r_new, w, *fixed, *arrived, *([adjoint] if colour == 1 else []))
    z, *sent = sent
    z, *sent = call(
        functools.partial(backward_kernel, swaps, tiles, 2),
        [kept] + pieces,
        [VMEM] * 2 + fixed_places + [VMEM] * n,
        scratch,
    )(w, z, *fixed, *exchange(sent))
    z, *sent, partial = call(
        functools.partial(backward_kernel, swaps, tiles, 1),
        [kept] + pieces + [vec(tiles, 16, 128)],
        [VMEM] * 2 + fixed_places + [VMEM] * (n + 3),
        scratch,
    )(w, z, *fixed, *exchange(sent), r_new, total, terms)
    sums = lax.all_to_all(partial, "gx", 0, 0, tiled=True)
    arrived = exchange(sent)
    off = call(load_kernel, [off_kept], [HBM, SMEM, VMEM], [pltpu.SemaphoreType.DMA((32,))], cost=10**8)(
        in_hbm(off_blocks), tables, arrived[0]
    )[0]
    z = call(
        functools.partial(backward_kernel, swaps, tiles, 0),
        [kept],
        [VMEM] * 2 + fixed_places + [VMEM] * n,
        scratch,
    )(w, z, off, *fixed[1:], *arrived)[0]
    block_vec = vec(32, 8, 128)
    x_new, q_new, d_new, scalars = call(
        functools.partial(last_kernel, count),
        [block_vec] * 3 + [vec(3, 8)],
        [VMEM] * 6 + [SMEM] * 3,
    )(sums, z, q, x_vec, d_vec, alpha, rho_prev, tau_prev, theta_prev)
    return (x_new, r_out, q_new, d_new, scalars)


def solution(mesh):
    blocks = P(("groups", "gx"))
    return jax.shard_map(
        per_device,
        mesh=mesh,
        in_specs=(blocks,) * 13 + (P("groups"),) * 3,
        out_specs=(blocks,) * 4 + (P(None, "groups"),),
        check_vma=False,
    )
```

```python
import functools

import jax
import jax.numpy as jnp
from jax import lax
from jax.experimental import pallas as pl
from jax.experimental.pallas import tpu as pltpu
from jax.sharding import PartitionSpec as P

F32 = jnp.float32
BF16 = jnp.bfloat16
VMEM = pltpu.VMEM
SMEM = pltpu.SMEM
HBM = pltpu.HBM
SIDE = 4
ORDER = (1, 2, 3, 0, 4, 5)
COUPLE = (8, 4, 2)
SOLVE = (16,)
LATE = 4
PART = 4
PARTS = (0, 16, 24, 32)


def swap_pairs(axis, stride, extent, phase, tiles):
    pairs = []
    for tile in range(tiles):
        place = tile // stride % extent
        up = place % 2 == phase
        other = place + 1 if up else place - 1
        if 0 <= other < extent:
            pairs.append((tile, tile + (other - place) * stride))
        elif axis == 0:
            pairs.append((tile, tile + (extent - 1 - 2 * place) * stride))
        else:
            pairs.append((tile, tile ^ 1))
    return pairs


def swaps_of(tiles):
    swaps = []
    for axis, (stride, extent) in enumerate(((1, SIDE), (SIDE, SIDE), (16, tiles // 16))):
        for phase in range(2 if extent > 2 else extent - 1):
            swaps.append((axis, phase, extent, swap_pairs(axis, stride, extent, phase, tiles)))
    return [swaps[i] for i in ORDER if i < len(swaps)]


def partner(axis, phase, extent):
    place = lax.rem(lax.axis_index("gx") // (1, SIDE, 16)[axis], extent)
    up = jnp.where(lax.rem(place, 2) == phase, 1, 0)
    other = place + 2 * up - 1
    return up, (other >= 0) & (other < extent)


def send_faces(swaps, state, faces, sent):
    for (axis, phase, extent, _), out in zip(swaps, sent):
        up, _ = partner(axis, phase, extent)
        face = 2 * axis + 1 - up
        for slot in range(0, 16, 2):
            two = [state[faces[face, 0, slot + j]] for j in range(2)]
            out[pl.ds(slot * 8, 16), :] = jnp.concatenate(two, axis=0).astype(BF16)


def own_blocks(state, extended):
    extended[pl.ds(0, 32)] = state[...].reshape(256, 128).astype(BF16).astype(F32).reshape(32, 8, 128)


def face_blocks(swaps, arrived, extended):
    for (axis, phase, extent, _), piece in zip(swaps, arrived):
        up, real = partner(axis, phase, extent)
        value = piece[pl.ds(0, 128), :].astype(F32).reshape(16, 8, 128)
        extended[pl.ds(32 + (2 * axis + up) * 16, 16)] = jnp.where(real, value, 0.0)


def extend(swaps, state, arrived, extended):
    own_blocks(state, extended)
    extended[pl.ds(32, 96)] = jnp.zeros((96, 8, 128), F32)
    face_blocks(swaps, arrived, extended)


def dot_t(left, right):
    return lax.dot_general(left, right, (((1,), (1,)), ((), ())), preferred_element_type=F32)


def coupled(block, extended, off, columns, first=()):
    vectors = [pair[0] for pair in first] + [extended[columns[k, block]] for k in range(9)]
    matrices = [pair[1] for pair in first] + [off[block, k] for k in range(9)]
    return dot_t(jnp.concatenate(vectors, axis=1).astype(BF16), jnp.concatenate(matrices, axis=1))


def solved(blocks, vectors, factor, straight, crossed):
    matrices = [factor[b] for b in blocks]
    pairs = range(0, len(blocks), 2)
    firsts = []
    for j in pairs:
        both = dot_t(jnp.concatenate(vectors[j : j + 2], axis=0).astype(BF16), jnp.concatenate(matrices[j : j + 2], axis=0))
        firsts += [both[:8, :128], both[8:, 128:]]
    even = lax.broadcasted_iota(jnp.int32, (8, 128), 1) % 2 == 0
    middles = []
    for b, first in zip(blocks, firsts):
        other = jnp.where(even, pltpu.roll(first, 127, 1), pltpu.roll(first, 1, 1))
        row = pl.ds(b, 1)
        middles.append(straight[row, :] * first + crossed[row, :] * other)
    values = []
    for j in pairs:
        left = jnp.concatenate(middles[j : j + 2], axis=0).astype(BF16)
        both = jnp.dot(left, jnp.concatenate(matrices[j : j + 2], axis=1), preferred_element_type=F32)
        values += [both[:8, :128], both[8:, 128:]]
    return values


def load_kernel(off_hbm, tables, after, off, sems):
    count = tables[4, 0]

    def copy(place):
        block = tables[0, place]
        return pltpu.make_async_copy(off_hbm.at[block], off.at[block], sems.at[place])

    lax.fori_loop(0, count, lambda place, carry: (copy(place).start(), carry)[1], 0)
    lax.fori_loop(0, count, lambda place, carry: (copy(place).wait(), carry)[1], 0)


def for_colour(colour, tables, sizes, body):
    count = tables[4, colour]
    done = 0
    for size in sizes:
        left = count - done
        groups = (left + size - 1) // size if size == sizes[-1] else left // size

        def step(group, carry, done=done, size=size):
            body([tables[colour, done + group * size + j] for j in range(size)])
            return carry

        lax.fori_loop(0, groups, step, 0)
        done = done + groups * size


def first_kernel(swaps, q_hbm, faces_hbm, colours_hbm, q, faces, *refs):
    sent, (colours, sems) = refs[:-2], refs[-2:]
    copies = [
        pltpu.make_async_copy(faces_hbm, faces, sems.at[0]),
        pltpu.make_async_copy(q_hbm, q, sems.at[1]),
        pltpu.make_async_copy(colours_hbm, colours, sems.at[2]),
    ]
    for copy in copies:
        copy.start()
    for copy in copies:
        copy.wait()
    send_faces(swaps, q, faces, sent)
    lane = lax.broadcasted_iota(jnp.int32, (16, 128), 1)
    for (axis, phase, extent, _), out in zip(swaps, sent):
        up, _ = partner(axis, phase, extent)
        face = 2 * axis + 1 - up
        listed = jnp.zeros((16, 128), jnp.int32)
        for slot in range(16):
            listed = jnp.where(lane == slot, colours[faces[face, 0, slot]], listed)
        out[pl.ds(128, 16), :] = listed.astype(F32).astype(BF16)


def setup_kernel(
    off_hbm, columns_hbm, colours_hbm, diag_ref, off_ref, pairs_ref, off, columns, tables, straight, crossed, colours, sems
):
    loads = [
        pltpu.make_async_copy(colours_hbm, colours, sems.at[0]),
        pltpu.make_async_copy(columns_hbm, columns, sems.at[1]),
        pltpu.make_async_copy(off_hbm.at[pl.ds(0, PARTS[1])], off.at[pl.ds(0, PARTS[1])], sems.at[2]),
    ]
    for load in loads:
        load.start()
    pair = lax.broadcasted_iota(jnp.int32, (64, 128), 0)
    lane = lax.broadcasted_iota(jnp.int32, (64, 128), 1)
    spread = jnp.where(lane // 2 == pair, 1.0, 0.0).astype(F32)
    cross = jnp.dot(off_ref[...], spread, precision=lax.Precision.HIGHEST, preferred_element_type=F32)
    paired = jnp.dot(pairs_ref[...].astype(F32), spread, precision=lax.Precision.HIGHEST, preferred_element_type=F32)
    own = diag_ref[...]
    even = lax.broadcasted_iota(jnp.int32, own.shape, 1) % 2 == 0
    other = jnp.where(even, pltpu.roll(own, 127, 1), pltpu.roll(own, 1, 1))
    det = own * other - cross * cross
    straight[...] = jnp.where(paired > 0.5, other / det, 1.0 / own)
    crossed[...] = jnp.where(paired > 0.5, -cross / det, 0.0)
    loads[0].wait()
    for colour in range(4):
        count = jnp.int32(0)
        for block in range(32):
            tables[colour, count] = block
            count = count + jnp.where(colours[block] == colour, 1, 0)
        last = tables[colour, jnp.maximum(count - 1, 0)]
        for j in range(16):
            tables[colour, count + j] = last
        tables[4, colour] = count
    for load in loads[1:]:
        load.wait()


def image_kernel(swaps, tiles, q, diag, off_hbm, off_in, columns, *refs):
    n = len(swaps)
    arrived, (off, image, partial, remote, extended, listed, sems) = refs[:n], refs[n:]
    loads = [None]
    for start, end in zip(PARTS[1:], PARTS[2:]):
        rows = pl.ds(start, end - start)
        loads.append(pltpu.make_async_copy(off_hbm.at[rows], off.at[rows], sems.at[len(loads) - 1]))
        loads[-1].start()
    listed[...] = jnp.full((8, 128), -1, jnp.int32)
    for (axis, phase, extent, _), piece in zip(swaps, arrived):
        up, real = partner(axis, phase, extent)
        found = piece[pl.ds(128, 16), :].astype(F32)[:1].astype(jnp.int32)
        listed[pl.ds(2 * axis + up, 1), :] = jnp.where(real, found, -1)
    colours = pltpu.make_async_copy(listed, remote, sems.at[len(loads) - 1])
    colours.start()
    extend(swaps, q, arrived, extended)

    total = jnp.zeros((8, 128), F32)
    for load, start, end in zip(loads, PARTS, PARTS[1:]):
        if load is not None:
            load.wait()
        blocks = range(start, end)
        values = [coupled(b, extended, off, columns, [(extended[b], diag[b])]) for b in blocks]
        for b, value in zip(blocks, values):
            image[b] = value
            total = total + q[b] * value
    for tile in range(tiles):
        partial[tile] = total
    colours.wait()


def column_of(values):
    row = lax.broadcasted_iota(jnp.int32, (8, 128), 0)
    out = jnp.zeros((8, 128), F32)
    for n in range(8):
        out = jnp.where(row == n, values[n], out)
    return out


def start_kernel(
    swaps, count, sums, r_ref, image, rho, factor, straight, crossed, tables, faces, r_new, w, alpha, *sent
):
    sigma = jnp.sum(jnp.sum(sums[...], axis=0), axis=1, keepdims=True) / count
    sigma = jnp.where(sigma >= 0, jnp.maximum(sigma, 0.5), jnp.minimum(sigma, -0.5))
    step_size = column_of(rho) / sigma
    alpha[...] = step_size
    new = r_ref[...] - step_size[None] * image[...]
    r_new[...] = new
    w[...] = jnp.zeros_like(w)

    def body(blocks):
        for b, value in zip(blocks, solved(blocks, [r_new[b] for b in blocks], factor, straight, crossed)):
            w[b] = value

    for_colour(0, tables, SOLVE, body)
    send_faces(swaps, w, faces, sent)


def adjoint_kernel(r_new, w, off, columns, tables, adjoint, terms, r_out):
    new = r_new[...]
    r_out[...] = new
    terms[pl.ds(0, 8), :] = jnp.sum(new * w[...], axis=0)
    terms[pl.ds(8, 8), :] = jnp.sum(new * new, axis=0)
    adjoint[...] = jnp.zeros_like(adjoint)
    count = tables[4, 0]

    def step(group, carry):
        products = []
        for j in range(PART):
            place = group * PART + j
            block = tables[0, place]
            vector = jnp.where(place < count, w[block], 0.0)
            high = vector.astype(BF16)
            low = (vector - high.astype(F32)).astype(BF16)
            matrix = jnp.concatenate([off[block, k] for k in range(9)], axis=1)
            both = jnp.dot(jnp.concatenate([high, low], axis=0), matrix, preferred_element_type=F32)
            products.append((block, both[:8] + both[8:]))
        for block, product in products:
            for k in range(9):
                column = columns[k, block]
                adjoint[column] = adjoint[column] + product[:, k * 128 : k * 128 + 128]
        return carry

    lax.fori_loop(0, (count + PART - 1) // PART, step, 0)


def gather_kernel(swaps, adjoint, faces, *refs):
    arrived, total = refs[:-1], refs[-1]
    total[...] = adjoint[pl.ds(0, 32)]
    for (axis, phase, extent, _), piece in zip(swaps, arrived):
        up, real = partner(axis, phase, extent)
        face = 2 * axis + 1 - up
        value = piece[pl.ds(128, 128), :].astype(F32).reshape(16, 8, 128)
        value = jnp.where(real, value, 0.0)
        for slot in range(16):
            block = faces[face, 0, slot]
            total[block] = total[block] + value[slot]


def early_kernel(colour, wanted, *refs):
    state, off, columns, tables, remote, extended, rest, late = refs[-8:]
    if len(refs) == 8:
        extended[pl.ds(32, 96)] = jnp.zeros((96, 8, 128), F32)
    own_blocks(state, extended)

    def couple(blocks):
        for b, value in zip(blocks, [coupled(b, extended, off, columns) for b in blocks]):
            rest[b] = value

    for_colour(colour, tables, COUPLE, couple)

    def note(place, found):
        block = tables[colour, place]
        for k in range(9):
            column = columns[k, block]
            slot = jnp.maximum(column - 32, 0)
            hit = (column >= 32) & (remote[slot >> 4, slot & 15] == wanted)
            late[found >> 7, found & 127] = block * 16 + k
            found = found + jnp.where(hit, 1, 0)
        return found

    found = lax.fori_loop(0, tables[4, colour], note, jnp.int32(0))
    for j in range(LATE):
        late[(found + j) >> 7, (found + j) & 127] = 0
    late[3, 0] = found


def couple_late(swaps, arrived, extended, rest, off, columns, late):
    face_blocks(swaps, arrived, extended)
    found = late[3, 0]

    def step(group, carry):
        products = []
        for j in range(LATE):
            place = group * LATE + j
            code = late[place >> 7, place & 127]
            block, k = code >> 4, code & 15
            vector = jnp.where(place < found, extended[columns[k, block]], 0.0)
            products.append((block, dot_t(vector.astype(BF16), off[block, k])))
        for block, product in products:
            rest[block] = rest[block] + product
        return carry

    lax.fori_loop(0, (found + LATE - 1) // LATE, step, 0)


def forward_kernel(swaps, colour, _, __, r_new, w_in, off, factor, straight, crossed, columns, tables, faces, late, *refs):
    n = len(swaps)
    arrived, others = refs[:n], refs[n:]
    if colour == 1:
        adjoint, others = others[0], others[1:]
    extended, rest, w, sent = others[0], others[1], others[2], others[3:]
    w[...] = w_in[...]
    couple_late(swaps, arrived, extended, rest, off, columns, late)

    def solve(blocks):
        for b, value in zip(blocks, solved(blocks, [r_new[b] - rest[b] for b in blocks], factor, straight, crossed)):
            w[b] = value

    for_colour(colour, tables, SOLVE, solve)
    if colour == 3:
        z = sent[0]
        z[...] = jnp.zeros_like(z)

        def copy(blocks):
            for b in blocks:
                z[b] = w[b]

        for_colour(3, tables, COUPLE, copy)
        send_faces(swaps, z, faces, sent[1:])
    else:
        send_faces(swaps, w, faces, sent)
    if colour == 1:
        for (axis, phase, extent, _), out in zip(swaps, sent):
            up, _ = partner(axis, phase, extent)
            value = adjoint[pl.ds(32 + (2 * axis + up) * 16, 16)]
            out[pl.ds(128, 128), :] = value.reshape(128, 128).astype(BF16)


def backward_kernel(swaps, tiles, colour, _, __, w, z_in, off, factor, straight, crossed, columns, tables, faces, late, *refs):
    n = len(swaps)
    arrived, others = refs[:n], refs[n:]
    if colour == 1:
        r_new, total, terms, partial = others[0], others[1], others[2], others[-1]
        others = others[3:-1]
    extended, rest, z, sent = others[0], others[1], others[2], others[3:]
    z[...] = z_in[...]
    couple_late(swaps, arrived, extended, rest, off, columns, late)

    def solve(blocks):
        for b, value in zip(blocks, solved(blocks, [rest[b] for b in blocks], factor, straight, crossed)):
            z[b] = w[b] - value

    for_colour(colour, tables, SOLVE, solve)
    if colour == 1:
        rho = terms[pl.ds(0, 8), :]
        for b in range(0, 32, 2):
            both = jnp.concatenate([z[b], z[b + 1]], axis=0)
            rounded = both.astype(BF16).astype(F32)
            part = jnp.concatenate([r_new[b], r_new[b + 1]], axis=0) * both
            part = part - jnp.concatenate([total[b], total[b + 1]], axis=0) * rounded
            rho = rho + part[:8] + part[8:]
        both = jnp.concatenate([rho, terms[pl.ds(8, 8), :]], axis=0)
        for tile in range(tiles):
            partial[tile] = both
    send_faces(swaps, z, faces, sent)


def final_kernel(swaps, w, z_in, off, factor, straight, crossed, columns, tables, faces, *refs):
    n = len(swaps)
    arrived, (z, extended, rest) = refs[:n], refs[n:]
    z[...] = z_in[...]
    extend(swaps, z_in, arrived, extended)

    def couple(blocks):
        for b, value in zip(blocks, [coupled(b, extended, off, columns) for b in blocks]):
            rest[b] = value

    def solve(blocks):
        for b, value in zip(blocks, solved(blocks, [rest[b] for b in blocks], factor, straight, crossed)):
            z[b] = w[b] - value

    for_colour(0, tables, COUPLE, couple)
    for_colour(0, tables, SOLVE, solve)


def last_kernel(count, sums, z, q_ref, x_ref, d_ref, alpha, rho, tau, theta_in, x_new, q_new, d_new, scalars):
    both = jnp.sum(jnp.sum(sums[...], axis=0), axis=1, keepdims=True) / count
    rho_new = both[:8] + jnp.zeros((8, 128), F32)
    norm = both[8:]
    tau_old = column_of(tau)
    theta_old = column_of(theta_in)
    theta = jnp.sqrt(norm + 1e-06) / tau_old
    csq = 1.0 / (1.0 + theta * theta)
    tau_new = tau_old * theta * jnp.sqrt(csq)
    beta = rho_new / column_of(rho)
    q_old = q_ref[...]
    d = (csq * theta_old * theta_old)[None] * d_ref[...] + (csq * alpha[...])[None] * q_old
    d_new[...] = d
    x_new[...] = x_ref[...] + d
    q_new[...] = z[...] + beta[None] * q_old
    row = lax.broadcasted_iota(jnp.int32, (8, 128), 0)
    lane = lax.broadcasted_iota(jnp.int32, (8, 128), 1)
    for index, value in enumerate((rho_new, tau_new, theta)):
        line = jnp.sum(jnp.where(row == lane, value, 0.0), axis=0, keepdims=True)
        scalars[pl.ds(index, 1), :] = line[:, :8]


def vec(*shape, dtype=F32):
    return jax.ShapeDtypeStruct(shape, dtype)


def call(body, outs, places, scratch=(), cost=0, aliases=None):
    return pl.pallas_call(
        body,
        out_shape=outs,
        in_specs=[pl.BlockSpec(memory_space=place) for place in places],
        out_specs=[pl.BlockSpec(memory_space=getattr(out, "memory_space", VMEM)) for out in outs],
        scratch_shapes=list(scratch),
        input_output_aliases=aliases or {},
        cost_estimate=pl.CostEstimate(flops=cost, bytes_accessed=0, transcendentals=0) if cost else None,
        compiler_params=pltpu.CompilerParams(vmem_limit_bytes=8 * 2**20),
    )


def in_hbm(array):
    return pltpu.with_memory_space_constraint(array, HBM)


def per_device(
    x_vec,
    r_vec,
    q_vec,
    d_vec,
    diag_blocks,
    off_blocks,
    columns,
    colours,
    factor_inv,
    pivot_diag,
    pivot_off,
    pivot_pairs,
    face_lists,
    rho_prev,
    tau_prev,
    theta_prev,
):
    tiles = lax.axis_size("gx")
    swaps = swaps_of(tiles)
    n = len(swaps)
    count = float(q_vec.shape[0] * q_vec.shape[2] * tiles)
    kept = VMEM((32, 8, 128), F32)
    pieces = [vec(128, 128, dtype=BF16)] * n
    scratch = [VMEM((128, 8, 128), F32), VMEM((32, 8, 128), F32)]
    off_kept = VMEM(off_blocks.shape, BF16)

    def exchange(sent):
        return [lax.ppermute(piece, "gx", swap[-1]) for piece, swap in zip(sent, swaps)]

    q, faces, *sent = call(
        functools.partial(first_kernel, swaps),
        [kept, SMEM((6, 1, 16), jnp.int32)] + [vec(144, 128, dtype=BF16)] * n,
        [HBM, HBM, HBM],
        [SMEM((32,), jnp.int32), pltpu.SemaphoreType.DMA((3,))],
        cost=10**10,
    )(in_hbm(q_vec), in_hbm(face_lists.transpose(1, 0, 2)), in_hbm(colours))
    arrived = exchange(sent)
    off, columns, tables, straight, crossed = call(
        setup_kernel,
        [off_kept, SMEM((9, 32), jnp.int32), SMEM((8, 128), jnp.int32), vec(32, 128), vec(32, 128)],
        [HBM, HBM, HBM, VMEM, VMEM, VMEM],
        [SMEM((32,), jnp.int32), pltpu.SemaphoreType.DMA((3,))],
    )(off_blocks, in_hbm(columns.T), in_hbm(colours), pivot_diag, pivot_off, pivot_pairs)
    off, image, partial, remote = call(
        functools.partial(image_kernel, swaps, tiles),
        [off_kept, kept, vec(tiles, 8, 128), SMEM((8, 128), jnp.int32)],
        [VMEM, VMEM, HBM, VMEM, SMEM] + [VMEM] * n,
        [scratch[0], VMEM((8, 128), jnp.int32), pltpu.SemaphoreType.DMA((4,))],
        aliases={3: 0},
    )(q, diag_blocks, off_blocks, off, columns, *arrived)
    sums = lax.all_to_all(partial, "gx", 0, 0, tiled=True)
    r_new, w, alpha, *sent = call(
        functools.partial(start_kernel, swaps, count),
        [kept, kept, vec(8, 128)] + pieces,
        [VMEM] * 3 + [SMEM] + [VMEM] * 3 + [SMEM] * 2,
    )(sums, r_vec, image, rho_prev, factor_inv, straight, crossed, tables, faces)
    fixed = (off, factor_inv, straight, crossed, columns, tables, faces)
    fixed_places = [VMEM] * 4 + [SMEM] * 3
    adjoint, terms, r_out = call(
        adjoint_kernel,
        [VMEM((128, 8, 128), F32), VMEM((16, 128), F32), vec(32, 8, 128)],
        [VMEM] * 3 + [SMEM] * 2,
        cost=10**8,
    )(r_new, w, off, columns, tables)
    long = [VMEM((128, 8, 128), F32), kept]

    def early(colour, wanted, state, extended):
        given = [] if extended is None else [extended]
        return call(
            functools.partial(early_kernel, colour, wanted),
            long + [SMEM((4, 128), jnp.int32)],
            [VMEM] * (len(given) + 2) + [SMEM] * 3,
            cost=10**8,
            aliases={0: 0} if given else None,
        )(*given, state, off, columns, tables, remote)

    extended = None
    for colour in (1, 2, 3):
        arrived = exchange(sent)
        extended, rest, late = early(colour, colour - 1, w, extended)
        if colour == 2:
            total = call(functools.partial(gather_kernel, swaps), [kept], [VMEM, SMEM] + [VMEM] * n, cost=10**8)(
                adjoint, faces, *arrived
            )[0]
        extended, _, w, *sent = call(
            functools.partial(forward_kernel, swaps, colour),
            long + [kept] * (2 if colour == 3 else 1) + ([vec(256, 128, dtype=BF16)] * n if colour == 1 else pieces),
            [VMEM] * 4 + fixed_places + [SMEM] + [VMEM] * (n + 1 if colour == 1 else n),
            aliases={0: 0, 1: 1},
        )(extended, rest, r_new, w, *fixed, late, *arrived, *([adjoint] if colour == 1 else []))
    z, *sent = sent
    arrived = exchange(sent)
    extended, rest, late = early(2, 3, z, None)
    extended, _, z, *sent = call(
        functools.partial(backward_kernel, swaps, tiles, 2),
        long + [kept] + pieces,
        [VMEM] * 4 + fixed_places + [SMEM] + [VMEM] * n,
        aliases={0: 0, 1: 1},
    )(extended, rest, w, z, *fixed, late, *arrived)
    arrived = exchange(sent)
    extended, rest, late = early(1, 2, z, extended)
    _, _, z, *sent, partial = call(
        functools.partial(backward_kernel, swaps, tiles, 1),
        long + [kept] + pieces + [vec(tiles, 16, 128)],
        [VMEM] * 4 + fixed_places + [SMEM] + [VMEM] * (n + 3),
        aliases={0: 0, 1: 1},
    )(extended, rest, w, z, *fixed, late, *arrived, r_new, total, terms)
    sums = lax.all_to_all(partial, "gx", 0, 0, tiled=True)
    arrived = exchange(sent)
    off = call(load_kernel, [off_kept], [HBM, SMEM, VMEM], [pltpu.SemaphoreType.DMA((32,))], cost=10**8)(
        in_hbm(off_blocks), tables, arrived[0]
    )[0]
    z = call(
        functools.partial(final_kernel, swaps),
        [kept],
        [VMEM] * 2 + fixed_places + [VMEM] * n,
        scratch,
    )(w, z, off, *fixed[1:], *arrived)[0]
    block_vec = vec(32, 8, 128)
    x_new, q_new, d_new, scalars = call(
        functools.partial(last_kernel, count),
        [block_vec] * 3 + [vec(3, 8)],
        [VMEM] * 6 + [SMEM] * 3,
    )(sums, z, q, x_vec, d_vec, alpha, rho_prev, tau_prev, theta_prev)
    return (x_new, r_out, q_new, d_new, scalars)


def solution(mesh):
    blocks = P(("groups", "gx"))
    return jax.shard_map(
        per_device,
        mesh=mesh,
        in_specs=(blocks,) * 13 + (P("groups"),) * 3,
        out_specs=(blocks,) * 4 + (P(None, "groups"),),
        check_vma=False,
    )
```

```python
import functools

import jax
import jax.numpy as jnp
from jax import lax
from jax.experimental import pallas as pl
from jax.experimental.pallas import tpu as pltpu
from jax.sharding import PartitionSpec as P

F32 = jnp.float32
BF16 = jnp.bfloat16
VMEM = pltpu.VMEM
SMEM = pltpu.SMEM
HBM = pltpu.HBM
SIDE = 4
ORDER = (1, 2, 3, 0, 4, 5)
COUPLE = (8, 4, 2)
SOLVE = (16,)
LATE = 8
PART = 4
PARTS = (0, 16, 24, 32)


def swap_pairs(axis, stride, extent, phase, tiles):
    pairs = []
    for tile in range(tiles):
        place = tile // stride % extent
        up = place % 2 == phase
        other = place + 1 if up else place - 1
        if 0 <= other < extent:
            pairs.append((tile, tile + (other - place) * stride))
        elif axis == 0:
            pairs.append((tile, tile + (extent - 1 - 2 * place) * stride))
        else:
            pairs.append((tile, tile ^ 1))
    return pairs


def swaps_of(tiles):
    swaps = []
    for axis, (stride, extent) in enumerate(((1, SIDE), (SIDE, SIDE), (16, tiles // 16))):
        for phase in range(2 if extent > 2 else extent - 1):
            swaps.append((axis, phase, extent, swap_pairs(axis, stride, extent, phase, tiles)))
    return [swaps[i] for i in ORDER if i < len(swaps)]


def partner(axis, phase, extent):
    place = lax.rem(lax.axis_index("gx") // (1, SIDE, 16)[axis], extent)
    up = jnp.where(lax.rem(place, 2) == phase, 1, 0)
    other = place + 2 * up - 1
    return up, (other >= 0) & (other < extent)


def send_faces(swaps, state, faces, sent):
    for (axis, phase, extent, _), out in zip(swaps, sent):
        up, _ = partner(axis, phase, extent)
        face = 2 * axis + 1 - up
        for slot in range(0, 16, 2):
            two = [state[faces[face, 0, slot + j]] for j in range(2)]
            out[pl.ds(slot * 8, 16), :] = jnp.concatenate(two, axis=0).astype(BF16)


def own_blocks(state, extended):
    extended[pl.ds(0, 32)] = state[...].reshape(256, 128).astype(BF16).astype(F32).reshape(32, 8, 128)


def face_blocks(swaps, arrived, extended):
    for (axis, phase, extent, _), piece in zip(swaps, arrived):
        up, real = partner(axis, phase, extent)
        value = piece[pl.ds(0, 128), :].astype(F32).reshape(16, 8, 128)
        extended[pl.ds(32 + (2 * axis + up) * 16, 16)] = jnp.where(real, value, 0.0)


def extend(swaps, state, arrived, extended):
    own_blocks(state, extended)
    extended[pl.ds(32, 96)] = jnp.zeros((96, 8, 128), F32)
    face_blocks(swaps, arrived, extended)


def dot_t(left, right):
    return lax.dot_general(left, right, (((1,), (1,)), ((), ())), preferred_element_type=F32)


def coupled(block, extended, off, columns, first=()):
    vectors = [pair[0] for pair in first] + [extended[columns[k, block]] for k in range(9)]
    matrices = [pair[1] for pair in first] + [off[block, k] for k in range(9)]
    return dot_t(jnp.concatenate(vectors, axis=1).astype(BF16), jnp.concatenate(matrices, axis=1))


def solved(blocks, vectors, factor, straight, crossed):
    matrices = [factor[b] for b in blocks]
    pairs = range(0, len(blocks), 2)
    firsts = []
    for j in pairs:
        both = dot_t(jnp.concatenate(vectors[j : j + 2], axis=0).astype(BF16), jnp.concatenate(matrices[j : j + 2], axis=0))
        firsts += [both[:8, :128], both[8:, 128:]]
    even = lax.broadcasted_iota(jnp.int32, (8, 128), 1) % 2 == 0
    middles = []
    for b, first in zip(blocks, firsts):
        other = jnp.where(even, pltpu.roll(first, 127, 1), pltpu.roll(first, 1, 1))
        row = pl.ds(b, 1)
        middles.append(straight[row, :] * first + crossed[row, :] * other)
    values = []
    for j in pairs:
        left = jnp.concatenate(middles[j : j + 2], axis=0).astype(BF16)
        both = jnp.dot(left, jnp.concatenate(matrices[j : j + 2], axis=1), preferred_element_type=F32)
        values += [both[:8, :128], both[8:, 128:]]
    return values


def load_kernel(off_hbm, tables, r_new, after, off, r_out, sems):
    count = tables[4, 0]
    out = pltpu.make_async_copy(r_new, r_out, sems.at[32])

    def copy(place):
        block = tables[0, place]
        return pltpu.make_async_copy(off_hbm.at[block], off.at[block], sems.at[place])

    lax.fori_loop(0, count, lambda place, carry: (copy(place).start(), carry)[1], 0)
    out.start()
    lax.fori_loop(0, count, lambda place, carry: (copy(place).wait(), carry)[1], 0)
    out.wait()


def for_colour(colour, tables, sizes, body):
    count = tables[4, colour]
    done = 0
    for size in sizes:
        left = count - done
        groups = (left + size - 1) // size if size == sizes[-1] else left // size

        def step(group, carry, done=done, size=size):
            places = [done + group * size + j for j in range(size)]
            body([tables[colour, place] for place in places], places)
            return carry

        lax.fori_loop(0, groups, step, 0)
        done = done + groups * size


def first_kernel(swaps, q_hbm, faces_hbm, colours_hbm, q, faces, *refs):
    sent, (colours, sems) = refs[:-2], refs[-2:]
    copies = [
        pltpu.make_async_copy(faces_hbm, faces, sems.at[0]),
        pltpu.make_async_copy(q_hbm, q, sems.at[1]),
        pltpu.make_async_copy(colours_hbm, colours, sems.at[2]),
    ]
    for copy in copies:
        copy.start()
    for copy in copies:
        copy.wait()
    send_faces(swaps, q, faces, sent)
    lane = lax.broadcasted_iota(jnp.int32, (16, 128), 1)
    for (axis, phase, extent, _), out in zip(swaps, sent):
        up, _ = partner(axis, phase, extent)
        face = 2 * axis + 1 - up
        listed = jnp.zeros((16, 128), jnp.int32)
        for slot in range(16):
            listed = jnp.where(lane == slot, colours[faces[face, 0, slot]], listed)
        out[pl.ds(128, 16), :] = listed.astype(F32).astype(BF16)


def setup_kernel(
    off_hbm, columns_hbm, colours_hbm, diag_ref, off_ref, pairs_ref, off, columns, tables, straight, crossed, colours, sems
):
    loads = [
        pltpu.make_async_copy(colours_hbm, colours, sems.at[0]),
        pltpu.make_async_copy(columns_hbm, columns, sems.at[1]),
        pltpu.make_async_copy(off_hbm.at[pl.ds(0, PARTS[1])], off.at[pl.ds(0, PARTS[1])], sems.at[2]),
    ]
    for load in loads:
        load.start()
    pair = lax.broadcasted_iota(jnp.int32, (64, 128), 0)
    lane = lax.broadcasted_iota(jnp.int32, (64, 128), 1)
    spread = jnp.where(lane // 2 == pair, 1.0, 0.0).astype(F32)
    cross = jnp.dot(off_ref[...], spread, precision=lax.Precision.HIGHEST, preferred_element_type=F32)
    paired = jnp.dot(pairs_ref[...].astype(F32), spread, precision=lax.Precision.HIGHEST, preferred_element_type=F32)
    own = diag_ref[...]
    even = lax.broadcasted_iota(jnp.int32, own.shape, 1) % 2 == 0
    other = jnp.where(even, pltpu.roll(own, 127, 1), pltpu.roll(own, 1, 1))
    det = own * other - cross * cross
    straight[...] = jnp.where(paired > 0.5, other / det, 1.0 / own)
    crossed[...] = jnp.where(paired > 0.5, -cross / det, 0.0)
    loads[0].wait()
    for colour in range(4):
        count = jnp.int32(0)
        for block in range(32):
            tables[colour, count] = block
            count = count + jnp.where(colours[block] == colour, 1, 0)
        last = tables[colour, jnp.maximum(count - 1, 0)]
        for j in range(16):
            tables[colour, count + j] = last
        tables[4, colour] = count
    for load in loads[1:]:
        load.wait()


def image_kernel(swaps, tiles, q, diag, off_hbm, off_in, columns, *refs):
    n = len(swaps)
    arrived, (off, image, partial, remote, extended, listed, sems) = refs[:n], refs[n:]
    loads = [None]
    for start, end in zip(PARTS[1:], PARTS[2:]):
        rows = pl.ds(start, end - start)
        loads.append(pltpu.make_async_copy(off_hbm.at[rows], off.at[rows], sems.at[len(loads) - 1]))
        loads[-1].start()
    listed[...] = jnp.full((8, 128), -1, jnp.int32)
    for (axis, phase, extent, _), piece in zip(swaps, arrived):
        up, real = partner(axis, phase, extent)
        found = piece[pl.ds(128, 16), :].astype(F32)[:1].astype(jnp.int32)
        listed[pl.ds(2 * axis + up, 1), :] = jnp.where(real, found, -1)
    colours = pltpu.make_async_copy(listed, remote, sems.at[len(loads) - 1])
    colours.start()
    extend(swaps, q, arrived, extended)

    total = jnp.zeros((8, 128), F32)
    for load, start, end in zip(loads, PARTS, PARTS[1:]):
        if load is not None:
            load.wait()
        blocks = range(start, end)
        values = [coupled(b, extended, off, columns, [(extended[b], diag[b])]) for b in blocks]
        for b, value in zip(blocks, values):
            image[b] = value
            total = total + q[b] * value
    for tile in range(tiles):
        partial[tile] = total
    colours.wait()


def column_of(values):
    row = lax.broadcasted_iota(jnp.int32, (8, 128), 0)
    out = jnp.zeros((8, 128), F32)
    for n in range(8):
        out = jnp.where(row == n, values[n], out)
    return out


def start_kernel(
    swaps, count, sums, r_ref, image, rho, factor, straight, crossed, tables, faces, r_new, w, alpha, *sent
):
    sigma = jnp.sum(jnp.sum(sums[...], axis=0), axis=1, keepdims=True) / count
    sigma = jnp.where(sigma >= 0, jnp.maximum(sigma, 0.5), jnp.minimum(sigma, -0.5))
    step_size = column_of(rho) / sigma
    alpha[...] = step_size
    new = r_ref[...] - step_size[None] * image[...]
    r_new[...] = new
    w[...] = jnp.zeros_like(w)

    def body(blocks, places):
        for b, value in zip(blocks, solved(blocks, [r_new[b] for b in blocks], factor, straight, crossed)):
            w[b] = value

    for_colour(0, tables, SOLVE, body)
    send_faces(swaps, w, faces, sent)


def adjoint_kernel(r_new, w, off, columns, tables, adjoint, terms):
    new = r_new[...]
    terms[pl.ds(0, 8), :] = jnp.sum(new * w[...], axis=0)
    terms[pl.ds(8, 8), :] = jnp.sum(new * new, axis=0)
    adjoint[...] = jnp.zeros_like(adjoint)
    count = tables[4, 0]

    def step(group, carry):
        products = []
        for j in range(PART):
            place = group * PART + j
            block = tables[0, place]
            vector = jnp.where(place < count, w[block], 0.0)
            high = vector.astype(BF16)
            low = (vector - high.astype(F32)).astype(BF16)
            matrix = jnp.concatenate([off[block, k] for k in range(9)], axis=1)
            both = jnp.dot(jnp.concatenate([high, low], axis=0), matrix, preferred_element_type=F32)
            products.append((block, both[:8] + both[8:]))
        for block, product in products:
            for k in range(9):
                column = columns[k, block]
                adjoint[column] = adjoint[column] + product[:, k * 128 : k * 128 + 128]
        return carry

    lax.fori_loop(0, (count + PART - 1) // PART, step, 0)


def gather_kernel(swaps, adjoint, faces, *refs):
    arrived, total = refs[:-1], refs[-1]
    total[...] = adjoint[pl.ds(0, 32)]
    for (axis, phase, extent, _), piece in zip(swaps, arrived):
        up, real = partner(axis, phase, extent)
        face = 2 * axis + 1 - up
        value = piece[pl.ds(128, 128), :].astype(F32).reshape(16, 8, 128)
        value = jnp.where(real, value, 0.0)
        for slot in range(16):
            block = faces[face, 0, slot]
            total[block] = total[block] + value[slot]


def early_kernel(colour, wanted, *refs):
    state, off, columns, tables, remote, extended, rest, late = refs[-8:]
    if len(refs) == 8:
        extended[pl.ds(32, 96)] = jnp.zeros((96, 8, 128), F32)
    own_blocks(state, extended)

    count = tables[4, colour]
    late[3, 0] = 0

    def couple(blocks, places):
        for b, value in zip(blocks, [coupled(b, extended, off, columns) for b in blocks]):
            rest[b] = value
        found = late[3, 0]
        for block, place in zip(blocks, places):
            for k in range(9):
                column = columns[k, block]
                slot = jnp.maximum(column - 32, 0)
                hit = (column >= 32) & (remote[slot >> 4, slot & 15] == wanted) & (place < count)
                late[found >> 7, found & 127] = block * 16 + k
                found = found + jnp.where(hit, 1, 0)
        late[3, 0] = found

    for_colour(colour, tables, COUPLE, couple)
    found = late[3, 0]
    for j in range(LATE):
        late[(found + j) >> 7, (found + j) & 127] = 0


def couple_late(swaps, arrived, extended, rest, off, columns, late):
    face_blocks(swaps, arrived, extended)
    found = late[3, 0]

    def step(group, carry):
        products = []
        for j in range(LATE):
            place = group * LATE + j
            code = late[place >> 7, place & 127]
            block, k = code >> 4, code & 15
            vector = jnp.where(place < found, extended[columns[k, block]], 0.0)
            products.append((block, dot_t(vector.astype(BF16), off[block, k])))
        for block, product in products:
            rest[block] = rest[block] + product
        return carry

    lax.fori_loop(0, (found + LATE - 1) // LATE, step, 0)


def forward_kernel(swaps, colour, _, __, r_new, w_in, off, factor, straight, crossed, columns, tables, faces, late, *refs):
    n = len(swaps)
    arrived, others = refs[:n], refs[n:]
    if colour == 1:
        adjoint, others = others[0], others[1:]
    extended, rest, w, sent = others[0], others[1], others[2], others[3:]
    w[...] = w_in[...]
    couple_late(swaps, arrived, extended, rest, off, columns, late)

    def solve(blocks, places):
        for b, value in zip(blocks, solved(blocks, [r_new[b] - rest[b] for b in blocks], factor, straight, crossed)):
            w[b] = value

    for_colour(colour, tables, SOLVE, solve)
    if colour == 3:
        z = sent[0]
        z[...] = jnp.zeros_like(z)

        def copy(blocks, places):
            for b in blocks:
                z[b] = w[b]

        for_colour(3, tables, COUPLE, copy)
        send_faces(swaps, z, faces, sent[1:])
    else:
        send_faces(swaps, w, faces, sent)
    if colour == 1:
        for (axis, phase, extent, _), out in zip(swaps, sent):
            up, _ = partner(axis, phase, extent)
            value = adjoint[pl.ds(32 + (2 * axis + up) * 16, 16)]
            out[pl.ds(128, 128), :] = value.reshape(128, 128).astype(BF16)


def backward_kernel(swaps, tiles, colour, _, __, w, z_in, off, factor, straight, crossed, columns, tables, faces, late, *refs):
    n = len(swaps)
    arrived, others = refs[:n], refs[n:]
    if colour == 1:
        r_new, total, terms, partial = others[0], others[1], others[2], others[-1]
        others = others[3:-1]
    extended, rest, z, sent = others[0], others[1], others[2], others[3:]
    z[...] = z_in[...]
    couple_late(swaps, arrived, extended, rest, off, columns, late)

    def solve(blocks, places):
        for b, value in zip(blocks, solved(blocks, [rest[b] for b in blocks], factor, straight, crossed)):
            z[b] = w[b] - value

    for_colour(colour, tables, SOLVE, solve)
    if colour == 1:
        rho = terms[pl.ds(0, 8), :]
        for b in range(0, 32, 2):
            both = jnp.concatenate([z[b], z[b + 1]], axis=0)
            rounded = both.astype(BF16).astype(F32)
            part = jnp.concatenate([r_new[b], r_new[b + 1]], axis=0) * both
            part = part - jnp.concatenate([total[b], total[b + 1]], axis=0) * rounded
            rho = rho + part[:8] + part[8:]
        both = jnp.concatenate([rho, terms[pl.ds(8, 8), :]], axis=0)
        for tile in range(tiles):
            partial[tile] = both
    send_faces(swaps, z, faces, sent)


def final_kernel(swaps, w, z_in, off, factor, straight, crossed, columns, tables, faces, *refs):
    n = len(swaps)
    arrived, (z, extended, rest) = refs[:n], refs[n:]
    z[...] = z_in[...]
    extend(swaps, z_in, arrived, extended)

    def couple(blocks, places):
        for b, value in zip(blocks, [coupled(b, extended, off, columns) for b in blocks]):
            rest[b] = value

    def solve(blocks, places):
        for b, value in zip(blocks, solved(blocks, [rest[b] for b in blocks], factor, straight, crossed)):
            z[b] = w[b] - value

    for_colour(0, tables, COUPLE, couple)
    for_colour(0, tables, SOLVE, solve)


def last_kernel(count, sums, z, q_ref, x_ref, d_ref, alpha, rho, tau, theta_in, x_new, q_new, d_new, scalars):
    both = jnp.sum(jnp.sum(sums[...], axis=0), axis=1, keepdims=True) / count
    rho_new = both[:8] + jnp.zeros((8, 128), F32)
    norm = both[8:]
    tau_old = column_of(tau)
    theta_old = column_of(theta_in)
    theta = jnp.sqrt(norm + 1e-06) / tau_old
    csq = 1.0 / (1.0 + theta * theta)
    tau_new = tau_old * theta * jnp.sqrt(csq)
    beta = rho_new / column_of(rho)
    q_old = q_ref[...]
    d = (csq * theta_old * theta_old)[None] * d_ref[...] + (csq * alpha[...])[None] * q_old
    d_new[...] = d
    x_new[...] = x_ref[...] + d
    q_new[...] = z[...] + beta[None] * q_old
    row = lax.broadcasted_iota(jnp.int32, (8, 128), 0)
    lane = lax.broadcasted_iota(jnp.int32, (8, 128), 1)
    for index, value in enumerate((rho_new, tau_new, theta)):
        line = jnp.sum(jnp.where(row == lane, value, 0.0), axis=0, keepdims=True)
        scalars[pl.ds(index, 1), :] = line[:, :8]


def vec(*shape, dtype=F32):
    return jax.ShapeDtypeStruct(shape, dtype)


def call(body, outs, places, scratch=(), cost=0, aliases=None):
    return pl.pallas_call(
        body,
        out_shape=outs,
        in_specs=[pl.BlockSpec(memory_space=place) for place in places],
        out_specs=[pl.BlockSpec(memory_space=getattr(out, "memory_space", VMEM)) for out in outs],
        scratch_shapes=list(scratch),
        input_output_aliases=aliases or {},
        cost_estimate=pl.CostEstimate(flops=cost, bytes_accessed=0, transcendentals=0) if cost else None,
        compiler_params=pltpu.CompilerParams(vmem_limit_bytes=8 * 2**20),
    )


def in_hbm(array):
    return pltpu.with_memory_space_constraint(array, HBM)


def per_device(
    x_vec,
    r_vec,
    q_vec,
    d_vec,
    diag_blocks,
    off_blocks,
    columns,
    colours,
    factor_inv,
    pivot_diag,
    pivot_off,
    pivot_pairs,
    face_lists,
    rho_prev,
    tau_prev,
    theta_prev,
):
    tiles = lax.axis_size("gx")
    swaps = swaps_of(tiles)
    n = len(swaps)
    count = float(q_vec.shape[0] * q_vec.shape[2] * tiles)
    kept = VMEM((32, 8, 128), F32)
    pieces = [vec(128, 128, dtype=BF16)] * n
    scratch = [VMEM((128, 8, 128), F32), VMEM((32, 8, 128), F32)]
    off_kept = VMEM(off_blocks.shape, BF16)

    def exchange(sent):
        return [lax.ppermute(piece, "gx", swap[-1]) for piece, swap in zip(sent, swaps)]

    q, faces, *sent = call(
        functools.partial(first_kernel, swaps),
        [kept, SMEM((6, 1, 16), jnp.int32)] + [vec(144, 128, dtype=BF16)] * n,
        [HBM, HBM, HBM],
        [SMEM((32,), jnp.int32), pltpu.SemaphoreType.DMA((3,))],
        cost=10**10,
    )(in_hbm(q_vec), in_hbm(face_lists.transpose(1, 0, 2)), in_hbm(colours))
    arrived = exchange(sent)
    off, columns, tables, straight, crossed = call(
        setup_kernel,
        [off_kept, SMEM((9, 32), jnp.int32), SMEM((8, 128), jnp.int32), vec(32, 128), vec(32, 128)],
        [HBM, HBM, HBM, VMEM, VMEM, VMEM],
        [SMEM((32,), jnp.int32), pltpu.SemaphoreType.DMA((3,))],
    )(off_blocks, in_hbm(columns.T), in_hbm(colours), pivot_diag, pivot_off, pivot_pairs)
    off, image, partial, remote = call(
        functools.partial(image_kernel, swaps, tiles),
        [off_kept, kept, vec(tiles, 8, 128), SMEM((8, 128), jnp.int32)],
        [VMEM, VMEM, HBM, VMEM, SMEM] + [VMEM] * n,
        [scratch[0], VMEM((8, 128), jnp.int32), pltpu.SemaphoreType.DMA((4,))],
        aliases={3: 0},
    )(q, diag_blocks, off_blocks, off, columns, *arrived)
    sums = lax.all_to_all(partial, "gx", 0, 0, tiled=True)
    r_new, w, alpha, *sent = call(
        functools.partial(start_kernel, swaps, count),
        [kept, kept, vec(8, 128)] + pieces,
        [VMEM] * 3 + [SMEM] + [VMEM] * 3 + [SMEM] * 2,
    )(sums, r_vec, image, rho_prev, factor_inv, straight, crossed, tables, faces)
    fixed = (off, factor_inv, straight, crossed, columns, tables, faces)
    fixed_places = [VMEM] * 4 + [SMEM] * 3
    adjoint, terms = call(
        adjoint_kernel,
        [VMEM((128, 8, 128), F32), VMEM((16, 128), F32)],
        [VMEM] * 3 + [SMEM] * 2,
        cost=10**8,
    )(r_new, w, off, columns, tables)
    long = [VMEM((128, 8, 128), F32), kept]

    def early(colour, wanted, state, extended):
        given = [] if extended is None else [extended]
        return call(
            functools.partial(early_kernel, colour, wanted),
            long + [SMEM((4, 128), jnp.int32)],
            [VMEM] * (len(given) + 2) + [SMEM] * 3,
            cost=10**8,
            aliases={0: 0} if given else None,
        )(*given, state, off, columns, tables, remote)

    extended = None
    for colour in (1, 2, 3):
        arrived = exchange(sent)
        extended, rest, late = early(colour, colour - 1, w, extended)
        if colour == 2:
            total = call(functools.partial(gather_kernel, swaps), [kept], [VMEM, SMEM] + [VMEM] * n, cost=10**8)(
                adjoint, faces, *arrived
            )[0]
        extended, _, w, *sent = call(
            functools.partial(forward_kernel, swaps, colour),
            long + [kept] * (2 if colour == 3 else 1) + ([vec(256, 128, dtype=BF16)] * n if colour == 1 else pieces),
            [VMEM] * 4 + fixed_places + [SMEM] + [VMEM] * (n + 1 if colour == 1 else n),
            aliases={0: 0, 1: 1},
        )(extended, rest, r_new, w, *fixed, late, *arrived, *([adjoint] if colour == 1 else []))
    z, *sent = sent
    arrived = exchange(sent)
    extended, rest, late = early(2, 3, z, None)
    extended, _, z, *sent = call(
        functools.partial(backward_kernel, swaps, tiles, 2),
        long + [kept] + pieces,
        [VMEM] * 4 + fixed_places + [SMEM] + [VMEM] * n,
        aliases={0: 0, 1: 1},
    )(extended, rest, w, z, *fixed, late, *arrived)
    arrived = exchange(sent)
    extended, rest, late = early(1, 2, z, extended)
    _, _, z, *sent, partial = call(
        functools.partial(backward_kernel, swaps, tiles, 1),
        long + [kept] + pieces + [vec(tiles, 16, 128)],
        [VMEM] * 4 + fixed_places + [SMEM] + [VMEM] * (n + 3),
        aliases={0: 0, 1: 1},
    )(extended, rest, w, z, *fixed, late, *arrived, r_new, total, terms)
    sums = lax.all_to_all(partial, "gx", 0, 0, tiled=True)
    arrived = exchange(sent)
    off, r_out = call(
        load_kernel,
        [off_kept, HBM((32, 8, 128), F32)],
        [HBM, SMEM, VMEM, VMEM],
        [pltpu.SemaphoreType.DMA((33,))],
        cost=10**8,
    )(in_hbm(off_blocks), tables, r_new, arrived[0])
    z = call(
        functools.partial(final_kernel, swaps),
        [kept],
        [VMEM] * 2 + fixed_places + [VMEM] * n,
        scratch,
    )(w, z, off, *fixed[1:], *arrived)[0]
    block_vec = vec(32, 8, 128)
    x_new, q_new, d_new, scalars = call(
        functools.partial(last_kernel, count),
        [block_vec] * 3 + [vec(3, 8)],
        [VMEM] * 6 + [SMEM] * 3,
    )(sums, z, q, x_vec, d_vec, alpha, rho_prev, tau_prev, theta_prev)
    return (x_new, r_out, q_new, d_new, scalars)


def solution(mesh):
    blocks = P(("groups", "gx"))
    return jax.shard_map(
        per_device,
        mesh=mesh,
        in_specs=(blocks,) * 13 + (P("groups"),) * 3,
        out_specs=(blocks,) * 4 + (P(None, "groups"),),
        check_vma=False,
    )
```

```python
import functools

import jax
import jax.numpy as jnp
from jax import lax
from jax.experimental import pallas as pl
from jax.experimental.pallas import tpu as pltpu
from jax.sharding import PartitionSpec as P

F32 = jnp.float32
BF16 = jnp.bfloat16
VMEM = pltpu.VMEM
SMEM = pltpu.SMEM
HBM = pltpu.HBM
SIDE = 4
ORDER = (1, 2, 3, 0, 4, 5)
COUPLE = (8, 4, 2)
SOLVE = (16,)
LATE = 8
PART = 4
PARTS = (0, 16, 32)


def swap_pairs(axis, stride, extent, phase, tiles):
    pairs = []
    for tile in range(tiles):
        place = tile // stride % extent
        up = place % 2 == phase
        other = place + 1 if up else place - 1
        if 0 <= other < extent:
            pairs.append((tile, tile + (other - place) * stride))
        elif axis == 0:
            pairs.append((tile, tile + (extent - 1 - 2 * place) * stride))
        else:
            pairs.append((tile, tile ^ 1))
    return pairs


def swaps_of(tiles):
    swaps = []
    for axis, (stride, extent) in enumerate(((1, SIDE), (SIDE, SIDE), (16, tiles // 16))):
        for phase in range(2 if extent > 2 else extent - 1):
            swaps.append((axis, phase, extent, swap_pairs(axis, stride, extent, phase, tiles)))
    return [swaps[i] for i in ORDER if i < len(swaps)]


def partner(axis, phase, extent):
    place = lax.rem(lax.axis_index("gx") // (1, SIDE, 16)[axis], extent)
    up = jnp.where(lax.rem(place, 2) == phase, 1, 0)
    other = place + 2 * up - 1
    return up, (other >= 0) & (other < extent)


def send_faces(swaps, state, faces, sent):
    for (axis, phase, extent, _), out in zip(swaps, sent):
        up, _ = partner(axis, phase, extent)
        face = 2 * axis + 1 - up
        for slot in range(0, 16, 2):
            two = [state[faces[face, 0, slot + j]] for j in range(2)]
            out[pl.ds(slot * 8, 16), :] = jnp.concatenate(two, axis=0).astype(BF16)


def own_blocks(state, extended):
    extended[pl.ds(0, 32)] = state[...].reshape(256, 128).astype(BF16).astype(F32).reshape(32, 8, 128)


def face_blocks(swaps, arrived, extended):
    for (axis, phase, extent, _), piece in zip(swaps, arrived):
        up, real = partner(axis, phase, extent)
        value = piece[pl.ds(0, 128), :].astype(F32).reshape(16, 8, 128)
        extended[pl.ds(32 + (2 * axis + up) * 16, 16)] = jnp.where(real, value, 0.0)


def extend(swaps, state, arrived, extended):
    own_blocks(state, extended)
    extended[pl.ds(32, 96)] = jnp.zeros((96, 8, 128), F32)
    face_blocks(swaps, arrived, extended)


def dot_t(left, right):
    return lax.dot_general(left, right, (((1,), (1,)), ((), ())), preferred_element_type=F32)


def coupled(block, extended, off, columns, first=()):
    vectors = [pair[0] for pair in first] + [extended[columns[k, block]] for k in range(9)]
    matrices = [pair[1] for pair in first] + [off[block, k] for k in range(9)]
    return dot_t(jnp.concatenate(vectors, axis=1).astype(BF16), jnp.concatenate(matrices, axis=1))


def solved(blocks, vectors, factor, straight, crossed):
    matrices = [factor[b] for b in blocks]
    pairs = range(0, len(blocks), 2)
    firsts = []
    for j in pairs:
        both = dot_t(jnp.concatenate(vectors[j : j + 2], axis=0).astype(BF16), jnp.concatenate(matrices[j : j + 2], axis=0))
        firsts += [both[:8, :128], both[8:, 128:]]
    even = lax.broadcasted_iota(jnp.int32, (8, 128), 1) % 2 == 0
    middles = []
    for b, first in zip(blocks, firsts):
        other = jnp.where(even, pltpu.roll(first, 127, 1), pltpu.roll(first, 1, 1))
        row = pl.ds(b, 1)
        middles.append(straight[row, :] * first + crossed[row, :] * other)
    values = []
    for j in pairs:
        left = jnp.concatenate(middles[j : j + 2], axis=0).astype(BF16)
        both = jnp.dot(left, jnp.concatenate(matrices[j : j + 2], axis=1), preferred_element_type=F32)
        values += [both[:8, :128], both[8:, 128:]]
    return values


def load_kernel(off_hbm, tables, r_new, after, off, r_out, sems):
    count = tables[4, 0]
    out = pltpu.make_async_copy(r_new, r_out, sems.at[32])

    def copy(place):
        block = tables[0, place]
        return pltpu.make_async_copy(off_hbm.at[block], off.at[block], sems.at[place])

    lax.fori_loop(0, count, lambda place, carry: (copy(place).start(), carry)[1], 0)
    out.start()
    lax.fori_loop(0, count, lambda place, carry: (copy(place).wait(), carry)[1], 0)
    out.wait()


def for_colour(colour, tables, sizes, body):
    count = tables[4, colour]
    done = 0
    for size in sizes:
        left = count - done
        groups = (left + size - 1) // size if size == sizes[-1] else left // size

        def step(group, carry, done=done, size=size):
            places = [done + group * size + j for j in range(size)]
            body([tables[colour, place] for place in places], places)
            return carry

        lax.fori_loop(0, groups, step, 0)
        done = done + groups * size


def first_kernel(swaps, q_hbm, faces_hbm, colours_hbm, q, faces, *refs):
    sent, (colours, sems) = refs[:-2], refs[-2:]
    copies = [
        pltpu.make_async_copy(faces_hbm, faces, sems.at[0]),
        pltpu.make_async_copy(q_hbm, q, sems.at[1]),
        pltpu.make_async_copy(colours_hbm, colours, sems.at[2]),
    ]
    for copy in copies:
        copy.start()
    for copy in copies:
        copy.wait()
    send_faces(swaps, q, faces, sent)
    lane = lax.broadcasted_iota(jnp.int32, (16, 128), 1)
    for (axis, phase, extent, _), out in zip(swaps, sent):
        up, _ = partner(axis, phase, extent)
        face = 2 * axis + 1 - up
        listed = jnp.zeros((16, 128), jnp.int32)
        for slot in range(16):
            listed = jnp.where(lane == slot, colours[faces[face, 0, slot]], listed)
        out[pl.ds(128, 16), :] = listed.astype(F32).astype(BF16)


def setup_kernel(
    off_hbm, columns_hbm, colours_hbm, diag_ref, off_ref, pairs_ref, off, columns, tables, straight, crossed, colours, sems
):
    loads = [
        pltpu.make_async_copy(colours_hbm, colours, sems.at[0]),
        pltpu.make_async_copy(columns_hbm, columns, sems.at[1]),
        pltpu.make_async_copy(off_hbm.at[pl.ds(0, PARTS[1])], off.at[pl.ds(0, PARTS[1])], sems.at[2]),
    ]
    for load in loads:
        load.start()
    pair = lax.broadcasted_iota(jnp.int32, (64, 128), 0)
    lane = lax.broadcasted_iota(jnp.int32, (64, 128), 1)
    spread = jnp.where(lane // 2 == pair, 1.0, 0.0).astype(F32)
    cross = jnp.dot(off_ref[...], spread, precision=lax.Precision.HIGHEST, preferred_element_type=F32)
    paired = jnp.dot(pairs_ref[...].astype(F32), spread, precision=lax.Precision.HIGHEST, preferred_element_type=F32)
    own = diag_ref[...]
    even = lax.broadcasted_iota(jnp.int32, own.shape, 1) % 2 == 0
    other = jnp.where(even, pltpu.roll(own, 127, 1), pltpu.roll(own, 1, 1))
    det = own * other - cross * cross
    straight[...] = jnp.where(paired > 0.5, other / det, 1.0 / own)
    crossed[...] = jnp.where(paired > 0.5, -cross / det, 0.0)
    loads[0].wait()
    for colour in range(4):
        count = jnp.int32(0)
        for block in range(32):
            tables[colour, count] = block
            count = count + jnp.where(colours[block] == colour, 1, 0)
        last = tables[colour, jnp.maximum(count - 1, 0)]
        for j in range(16):
            tables[colour, count + j] = last
        tables[4, colour] = count
    for load in loads[1:]:
        load.wait()


def image_kernel(swaps, tiles, q, diag, off_hbm, off_in, columns, *refs):
    n = len(swaps)
    arrived, (off, image, partial, remote, extended, listed, sems) = refs[:n], refs[n:]
    loads = [None]
    for start, end in zip(PARTS[1:], PARTS[2:]):
        rows = pl.ds(start, end - start)
        loads.append(pltpu.make_async_copy(off_hbm.at[rows], off.at[rows], sems.at[len(loads) - 1]))
        loads[-1].start()
    listed[...] = jnp.full((8, 128), -1, jnp.int32)
    for (axis, phase, extent, _), piece in zip(swaps, arrived):
        up, real = partner(axis, phase, extent)
        found = piece[pl.ds(128, 16), :].astype(F32)[:1].astype(jnp.int32)
        listed[pl.ds(2 * axis + up, 1), :] = jnp.where(real, found, -1)
    colours = pltpu.make_async_copy(listed, remote, sems.at[len(loads) - 1])
    colours.start()
    extend(swaps, q, arrived, extended)

    total = jnp.zeros((8, 128), F32)
    for load, start, end in zip(loads, PARTS, PARTS[1:]):
        if load is not None:
            load.wait()
        blocks = range(start, end)
        values = [coupled(b, extended, off, columns, [(extended[b], diag[b])]) for b in blocks]
        for b, value in zip(blocks, values):
            image[b] = value
            total = total + q[b] * value
    for tile in range(tiles):
        partial[tile] = total
    colours.wait()


def column_of(values):
    row = lax.broadcasted_iota(jnp.int32, (8, 128), 0)
    out = jnp.zeros((8, 128), F32)
    for n in range(8):
        out = jnp.where(row == n, values[n], out)
    return out


def start_kernel(
    swaps, count, sums, r_ref, image, rho, factor, straight, crossed, tables, faces, r_new, w, alpha, *sent
):
    sigma = jnp.sum(jnp.sum(sums[...], axis=0), axis=1, keepdims=True) / count
    sigma = jnp.where(sigma >= 0, jnp.maximum(sigma, 0.5), jnp.minimum(sigma, -0.5))
    step_size = column_of(rho) / sigma
    alpha[...] = step_size
    new = r_ref[...] - step_size[None] * image[...]
    r_new[...] = new
    w[...] = jnp.zeros_like(w)

    def body(blocks, places):
        for b, value in zip(blocks, solved(blocks, [r_new[b] for b in blocks], factor, straight, crossed)):
            w[b] = value

    for_colour(0, tables, SOLVE, body)
    send_faces(swaps, w, faces, sent)


def adjoint_kernel(r_new, w, off, columns, tables, adjoint, terms):
    new = r_new[...]
    terms[pl.ds(0, 8), :] = jnp.sum(new * w[...], axis=0)
    terms[pl.ds(8, 8), :] = jnp.sum(new * new, axis=0)
    adjoint[...] = jnp.zeros_like(adjoint)
    count = tables[4, 0]

    def step(group, carry):
        products = []
        for j in range(PART):
            place = group * PART + j
            block = tables[0, place]
            vector = jnp.where(place < count, w[block], 0.0)
            high = vector.astype(BF16)
            low = (vector - high.astype(F32)).astype(BF16)
            matrix = jnp.concatenate([off[block, k] for k in range(9)], axis=1)
            both = jnp.dot(jnp.concatenate([high, low], axis=0), matrix, preferred_element_type=F32)
            products.append((block, both[:8] + both[8:]))
        for block, product in products:
            for k in range(9):
                column = columns[k, block]
                adjoint[column] = adjoint[column] + product[:, k * 128 : k * 128 + 128]
        return carry

    lax.fori_loop(0, (count + PART - 1) // PART, step, 0)


def gather_kernel(swaps, adjoint, faces, *refs):
    arrived, total = refs[:-1], refs[-1]
    total[...] = adjoint[pl.ds(0, 32)]
    for (axis, phase, extent, _), piece in zip(swaps, arrived):
        up, real = partner(axis, phase, extent)
        face = 2 * axis + 1 - up
        value = piece[pl.ds(128, 128), :].astype(F32).reshape(16, 8, 128)
        value = jnp.where(real, value, 0.0)
        for slot in range(16):
            block = faces[face, 0, slot]
            total[block] = total[block] + value[slot]


def early_kernel(colour, wanted, *refs):
    state, off, columns, tables, remote, extended, rest, late = refs[-8:]
    if len(refs) == 8:
        extended[pl.ds(32, 96)] = jnp.zeros((96, 8, 128), F32)
    own_blocks(state, extended)

    count = tables[4, colour]
    late[3, 0] = 0

    def couple(blocks, places):
        for b, value in zip(blocks, [coupled(b, extended, off, columns) for b in blocks]):
            rest[b] = value
        found = late[3, 0]
        for block, place in zip(blocks, places):
            for k in range(9):
                column = columns[k, block]
                slot = jnp.maximum(column - 32, 0)
                hit = (column >= 32) & (remote[slot >> 4, slot & 15] == wanted) & (place < count)
                late[found >> 7, found & 127] = block * 16 + k
                found = found + jnp.where(hit, 1, 0)
        late[3, 0] = found

    for_colour(colour, tables, COUPLE, couple)
    found = late[3, 0]
    for j in range(LATE):
        late[(found + j) >> 7, (found + j) & 127] = 0


def couple_late(swaps, arrived, extended, rest, off, columns, late):
    face_blocks(swaps, arrived, extended)
    found = late[3, 0]

    def step(group, carry):
        products = []
        for j in range(LATE):
            place = group * LATE + j
            code = late[place >> 7, place & 127]
            block, k = code >> 4, code & 15
            vector = jnp.where(place < found, extended[columns[k, block]], 0.0)
            products.append((block, dot_t(vector.astype(BF16), off[block, k])))
        for block, product in products:
            rest[block] = rest[block] + product
        return carry

    lax.fori_loop(0, (found + LATE - 1) // LATE, step, 0)


def forward_kernel(swaps, colour, _, __, r_new, w_in, off, factor, straight, crossed, columns, tables, faces, late, *refs):
    n = len(swaps)
    arrived, others = refs[:n], refs[n:]
    if colour == 1:
        adjoint, others = others[0], others[1:]
    extended, rest, w, sent = others[0], others[1], others[2], others[3:]
    couple_late(swaps, arrived, extended, rest, off, columns, late)

    def solve(blocks, places):
        for b, value in zip(blocks, solved(blocks, [r_new[b] - rest[b] for b in blocks], factor, straight, crossed)):
            w[b] = value

    for_colour(colour, tables, SOLVE, solve)
    if colour == 3:
        z = sent[0]
        z[...] = jnp.zeros_like(z)

        def copy(blocks, places):
            for b in blocks:
                z[b] = w[b]

        for_colour(3, tables, COUPLE, copy)
        send_faces(swaps, z, faces, sent[1:])
    else:
        send_faces(swaps, w, faces, sent)
    if colour == 1:
        for (axis, phase, extent, _), out in zip(swaps, sent):
            up, _ = partner(axis, phase, extent)
            value = adjoint[pl.ds(32 + (2 * axis + up) * 16, 16)]
            out[pl.ds(128, 128), :] = value.reshape(128, 128).astype(BF16)


def backward_kernel(swaps, tiles, colour, _, __, w, z_in, off, factor, straight, crossed, columns, tables, faces, late, *refs):
    n = len(swaps)
    arrived, others = refs[:n], refs[n:]
    if colour == 1:
        r_new, total, terms, partial = others[0], others[1], others[2], others[-1]
        others = others[3:-1]
    extended, rest, z, sent = others[0], others[1], others[2], others[3:]
    couple_late(swaps, arrived, extended, rest, off, columns, late)

    def solve(blocks, places):
        for b, value in zip(blocks, solved(blocks, [rest[b] for b in blocks], factor, straight, crossed)):
            z[b] = w[b] - value

    for_colour(colour, tables, SOLVE, solve)
    if colour == 1:
        rho = terms[pl.ds(0, 8), :]
        for b in range(0, 32, 2):
            both = jnp.concatenate([z[b], z[b + 1]], axis=0)
            rounded = both.astype(BF16).astype(F32)
            part = jnp.concatenate([r_new[b], r_new[b + 1]], axis=0) * both
            part = part - jnp.concatenate([total[b], total[b + 1]], axis=0) * rounded
            rho = rho + part[:8] + part[8:]
        both = jnp.concatenate([rho, terms[pl.ds(8, 8), :]], axis=0)
        for tile in range(tiles):
            partial[tile] = both
    send_faces(swaps, z, faces, sent)


def final_kernel(swaps, w, z_in, off, factor, straight, crossed, columns, tables, faces, *refs):
    n = len(swaps)
    arrived, (z, extended, rest) = refs[:n], refs[n:]
    extend(swaps, z_in, arrived, extended)

    def couple(blocks, places):
        for b, value in zip(blocks, [coupled(b, extended, off, columns) for b in blocks]):
            rest[b] = value

    def solve(blocks, places):
        for b, value in zip(blocks, solved(blocks, [rest[b] for b in blocks], factor, straight, crossed)):
            z[b] = w[b] - value

    for_colour(0, tables, COUPLE, couple)
    for_colour(0, tables, SOLVE, solve)


def last_kernel(count, sums, z, q_ref, x_ref, d_ref, alpha, rho, tau, theta_in, x_new, q_new, d_new, scalars):
    both = jnp.sum(jnp.sum(sums[...], axis=0), axis=1, keepdims=True) / count
    rho_new = both[:8] + jnp.zeros((8, 128), F32)
    norm = both[8:]
    tau_old = column_of(tau)
    theta_old = column_of(theta_in)
    theta = jnp.sqrt(norm + 1e-06) / tau_old
    csq = 1.0 / (1.0 + theta * theta)
    tau_new = tau_old * theta * jnp.sqrt(csq)
    beta = rho_new / column_of(rho)
    q_old = q_ref[...]
    d = (csq * theta_old * theta_old)[None] * d_ref[...] + (csq * alpha[...])[None] * q_old
    d_new[...] = d
    x_new[...] = x_ref[...] + d
    q_new[...] = z[...] + beta[None] * q_old
    row = lax.broadcasted_iota(jnp.int32, (8, 128), 0)
    lane = lax.broadcasted_iota(jnp.int32, (8, 128), 1)
    for index, value in enumerate((rho_new, tau_new, theta)):
        line = jnp.sum(jnp.where(row == lane, value, 0.0), axis=0, keepdims=True)
        scalars[pl.ds(index, 1), :] = line[:, :8]


def vec(*shape, dtype=F32):
    return jax.ShapeDtypeStruct(shape, dtype)


def call(body, outs, places, scratch=(), cost=0, aliases=None):
    return pl.pallas_call(
        body,
        out_shape=outs,
        in_specs=[pl.BlockSpec(memory_space=place) for place in places],
        out_specs=[pl.BlockSpec(memory_space=getattr(out, "memory_space", VMEM)) for out in outs],
        scratch_shapes=list(scratch),
        input_output_aliases=aliases or {},
        cost_estimate=pl.CostEstimate(flops=cost, bytes_accessed=0, transcendentals=0) if cost else None,
        compiler_params=pltpu.CompilerParams(vmem_limit_bytes=8 * 2**20),
    )


def in_hbm(array):
    return pltpu.with_memory_space_constraint(array, HBM)


def per_device(
    x_vec,
    r_vec,
    q_vec,
    d_vec,
    diag_blocks,
    off_blocks,
    columns,
    colours,
    factor_inv,
    pivot_diag,
    pivot_off,
    pivot_pairs,
    face_lists,
    rho_prev,
    tau_prev,
    theta_prev,
):
    tiles = lax.axis_size("gx")
    swaps = swaps_of(tiles)
    n = len(swaps)
    count = float(q_vec.shape[0] * q_vec.shape[2] * tiles)
    kept = VMEM((32, 8, 128), F32)
    pieces = [vec(128, 128, dtype=BF16)] * n
    scratch = [VMEM((128, 8, 128), F32), VMEM((32, 8, 128), F32)]
    off_kept = VMEM(off_blocks.shape, BF16)

    def exchange(sent):
        return [lax.ppermute(piece, "gx", swap[-1]) for piece, swap in zip(sent, swaps)]

    q, faces, *sent = call(
        functools.partial(first_kernel, swaps),
        [kept, SMEM((6, 1, 16), jnp.int32)] + [vec(144, 128, dtype=BF16)] * n,
        [HBM, HBM, HBM],
        [SMEM((32,), jnp.int32), pltpu.SemaphoreType.DMA((3,))],
        cost=10**10,
    )(in_hbm(q_vec), in_hbm(face_lists.transpose(1, 0, 2)), in_hbm(colours))
    arrived = exchange(sent)
    off, columns, tables, straight, crossed = call(
        setup_kernel,
        [off_kept, SMEM((9, 32), jnp.int32), SMEM((8, 128), jnp.int32), vec(32, 128), vec(32, 128)],
        [HBM, HBM, HBM, VMEM, VMEM, VMEM],
        [SMEM((32,), jnp.int32), pltpu.SemaphoreType.DMA((3,))],
    )(off_blocks, in_hbm(columns.T), in_hbm(colours), pivot_diag, pivot_off, pivot_pairs)
    off, image, partial, remote = call(
        functools.partial(image_kernel, swaps, tiles),
        [off_kept, kept, vec(tiles, 8, 128), SMEM((8, 128), jnp.int32)],
        [VMEM, VMEM, HBM, VMEM, SMEM] + [VMEM] * n,
        [scratch[0], VMEM((8, 128), jnp.int32), pltpu.SemaphoreType.DMA((4,))],
        aliases={3: 0},
    )(q, diag_blocks, off_blocks, off, columns, *arrived)
    sums = lax.all_to_all(partial, "gx", 0, 0, tiled=True)
    r_new, w, alpha, *sent = call(
        functools.partial(start_kernel, swaps, count),
        [kept, kept, vec(8, 128)] + pieces,
        [VMEM] * 3 + [SMEM] + [VMEM] * 3 + [SMEM] * 2,
    )(sums, r_vec, image, rho_prev, factor_inv, straight, crossed, tables, faces)
    fixed = (off, factor_inv, straight, crossed, columns, tables, faces)
    fixed_places = [VMEM] * 4 + [SMEM] * 3
    adjoint, terms = call(
        adjoint_kernel,
        [VMEM((128, 8, 128), F32), VMEM((16, 128), F32)],
        [VMEM] * 3 + [SMEM] * 2,
        cost=10**8,
    )(r_new, w, off, columns, tables)
    long = [VMEM((128, 8, 128), F32), kept]

    def early(colour, wanted, state, extended):
        given = [] if extended is None else [extended]
        return call(
            functools.partial(early_kernel, colour, wanted),
            long + [SMEM((4, 128), jnp.int32)],
            [VMEM] * (len(given) + 2) + [SMEM] * 3,
            cost=10**8,
            aliases={0: 0} if given else None,
        )(*given, state, off, columns, tables, remote)

    extended = None
    for colour in (1, 2, 3):
        arrived = exchange(sent)
        extended, rest, late = early(colour, colour - 1, w, extended)
        if colour == 2:
            total = call(functools.partial(gather_kernel, swaps), [kept], [VMEM, SMEM] + [VMEM] * n, cost=10**8)(
                adjoint, faces, *arrived
            )[0]
        extended, _, w, *sent = call(
            functools.partial(forward_kernel, swaps, colour),
            long + [kept] * (2 if colour == 3 else 1) + ([vec(256, 128, dtype=BF16)] * n if colour == 1 else pieces),
            [VMEM] * 4 + fixed_places + [SMEM] + [VMEM] * (n + 1 if colour == 1 else n),
            aliases={0: 0, 1: 1, 3: 2},
        )(extended, rest, r_new, w, *fixed, late, *arrived, *([adjoint] if colour == 1 else []))
    z, *sent = sent
    arrived = exchange(sent)
    extended, rest, late = early(2, 3, z, None)
    extended, _, z, *sent = call(
        functools.partial(backward_kernel, swaps, tiles, 2),
        long + [kept] + pieces,
        [VMEM] * 4 + fixed_places + [SMEM] + [VMEM] * n,
        aliases={0: 0, 1: 1, 3: 2},
    )(extended, rest, w, z, *fixed, late, *arrived)
    arrived = exchange(sent)
    extended, rest, late = early(1, 2, z, extended)
    _, _, z, *sent, partial = call(
        functools.partial(backward_kernel, swaps, tiles, 1),
        long + [kept] + pieces + [vec(tiles, 16, 128)],
        [VMEM] * 4 + fixed_places + [SMEM] + [VMEM] * (n + 3),
        aliases={0: 0, 1: 1, 3: 2},
    )(extended, rest, w, z, *fixed, late, *arrived, r_new, total, terms)
    sums = lax.all_to_all(partial, "gx", 0, 0, tiled=True)
    arrived = exchange(sent)
    off, r_out = call(
        load_kernel,
        [off_kept, HBM((32, 8, 128), F32)],
        [HBM, SMEM, VMEM, VMEM],
        [pltpu.SemaphoreType.DMA((33,))],
        cost=10**8,
    )(in_hbm(off_blocks), tables, r_new, arrived[0])
    z = call(
        functools.partial(final_kernel, swaps),
        [kept],
        [VMEM] * 2 + fixed_places + [VMEM] * n,
        scratch,
        aliases={1: 0},
    )(w, z, off, *fixed[1:], *arrived)[0]
    block_vec = vec(32, 8, 128)
    x_new, q_new, d_new, scalars = call(
        functools.partial(last_kernel, count),
        [block_vec] * 3 + [vec(3, 8)],
        [VMEM] * 6 + [SMEM] * 3,
    )(sums, z, q, x_vec, d_vec, alpha, rho_prev, tau_prev, theta_prev)
    return (x_new, r_out, q_new, d_new, scalars)


def solution(mesh):
    blocks = P(("groups", "gx"))
    return jax.shard_map(
        per_device,
        mesh=mesh,
        in_specs=(blocks,) * 13 + (P("groups"),) * 3,
        out_specs=(blocks,) * 4 + (P(None, "groups"),),
        check_vma=False,
    )
```
